128 devices in a mesh: prefix: 16 (over z, y), req: 8 (over x, core).
Axes of the slice: x: 4, y: 4, z: 4, core: 2. Of those that a mesh axis runs over, the one named last changes fastest.
Arguments:
- queries: bfloat16 [2048, 2, 8192], P(('prefix', 'req')), may hold values from -12 to 12
- new_keys: bfloat16 [2048, 2, 512], P(('prefix', 'req')), may hold values from -6 to 6
- new_values: bfloat16 [2048, 2, 512], P(('prefix', 'req')), may hold values from -6 to 6
- suffix_keys: bfloat16 [2048, 256, 512], P(('prefix', 'req')), may hold values from -6 to 6
- suffix_values: bfloat16 [2048, 256, 512], P(('prefix', 'req')), may hold values from -6 to 6
- suffix_lengths: int32 [2048], P(('prefix', 'req')), may hold values from 1 to 256
- prefix_of: int32 [2048], P(('prefix', 'req')), may hold values from 0 to 15, as said below
- prefix_keys: bfloat16 [16, 8192, 512], P('prefix', 'req'), may hold values from -12 to 12
- prefix_values: bfloat16 [16, 8192, 512], P('prefix', 'req'), may hold values from -6 to 6
- prefix_lengths: int32 [16], P('prefix'), may hold values from 2048 to 8192
Outputs:
- attended: bfloat16 [2048, 2, 8192], P(('prefix', 'req'))
The draws below stay inside these ranges and needn't reach their ends.
Inputs may be any that keep to these rules, and one draw needn't show every extreme that they name: `prefix_of`: among the 16 requests of one device no prefix appears more than 2 times.
All inputs are finite; a program needn't handle non-finite values.
Results may differ from the reference program's by a relative error of at most 0.0056.
Values may be sent and summed in bfloat16 or wider, within the bound.
No kernel may reach another device: no remote copies, remote signals or barrier semaphores. Data moves between devices by JAX's collectives and lax.ppermute only.
A program may use at most 192 MiB of HBM per device.

```python
import jax
import jax.numpy as jnp
from jax import lax

H = 64
KVH = 4
HD = 128
REQ_DEV = 16
PLEN = 8192
SLEN = 256
STEPS = 2
CAP = 2
PREFIXES = 16
REQUESTS = 2048
N_REQ = 8


def draw_queries(key, part):
    key = jax.random.fold_in(key, 1)
    values = jnp.clip(jax.random.normal(key, (REQUESTS, STEPS, H * HD), jnp.float32), -6.0, 6.0)
    return values.astype(jnp.bfloat16)


def draw_prefix_keys(key, part):
    key = jax.random.fold_in(key, 2)
    values = jnp.clip(jax.random.normal(key, (PREFIXES, PLEN, KVH * HD), jnp.float32), -6.0, 6.0)
    return values.astype(jnp.bfloat16)


def draw_prefix_of(key, part):
    key = jax.random.fold_in(key, 5)
    hottest = jax.random.randint(key, (), 0, PREFIXES)
    spare = jnp.arange((PREFIXES - 1) * CAP, dtype=jnp.int32) // CAP
    spare = spare + (spare >= hottest).astype(jnp.int32)

    def one_block(index):
        block_key = jax.random.fold_in(key, index + 1)
        order = jax.random.permutation(block_key, (PREFIXES - 1) * CAP)
        picked = spare[order[:REQ_DEV - CAP]]
        row_ids = jnp.concatenate([jnp.full((CAP,), hottest, jnp.int32), picked])
        return row_ids[jax.random.permutation(jax.random.fold_in(block_key, 7), REQ_DEV)]
    return jax.vmap(one_block)(jnp.arange(REQUESTS // REQ_DEV)).reshape(REQUESTS).astype(jnp.int32)


def draw_prefix_lengths(key, part):
    key = jax.random.fold_in(key, 6)
    lengths = jax.random.randint(key, (PREFIXES,), PLEN // 4, PLEN + 1)
    longest = jax.random.randint(jax.random.fold_in(key, 1), (), 0, PREFIXES)
    return lengths.at[longest].set(PLEN).astype(jnp.int32)


def draw_suffix_lengths(key, part):
    key = jax.random.fold_in(key, 7)
    lengths = jax.random.randint(key, (REQUESTS,), 1, SLEN + 1)
    longest = jax.random.randint(jax.random.fold_in(key, 1), (), 0, REQUESTS)
    return lengths.at[longest].set(SLEN).astype(jnp.int32)


def level_of(stream_key, extent, cuts, least, top_value):
    def one(dim, blocks):
        heights = jax.random.uniform(jax.random.fold_in(jax.random.fold_in(stream_key, 6), dim), (blocks,), jnp.float32, least / len(cuts), top_value / len(cuts))
        return jnp.repeat(jnp.exp(heights), extent[dim] // blocks).reshape((-1,) + (1,) * (len(extent) - dim - 1))

    level = one(*cuts[0])
    for cut in cuts[1:]:
        level = level * one(*cut)
    return level


def bell_draw(key, extent, width, reach, pieces=(), kind=jnp.bfloat16):
    level = level_of(key, extent, pieces, -0.22, 0.18) if pieces else 1.0
    entries = jax.random.normal(key, extent, jnp.float32) * width * level
    return jnp.minimum(jnp.maximum(entries, -reach), reach).astype(kind)


def setup_inputs(seed: int = 0) -> dict:
    splits = jax.random.split(jax.random.key(seed), 11)
    return {
        "queries": draw_queries(jax.random.fold_in(splits[10], 71), 0),
        "new_keys": bell_draw(splits[1], (REQUESTS, STEPS, KVH * HD), 1.0, 6.0, ((0, 128),)),
        "new_values": bell_draw(splits[2], (REQUESTS, STEPS, KVH * HD), 1.0, 6.0, ((0, 128),)),
        "suffix_keys": bell_draw(splits[3], (REQUESTS, SLEN, KVH * HD), 1.0, 6.0, ((0, 128),)),
        "suffix_values": bell_draw(splits[4], (REQUESTS, SLEN, KVH * HD), 1.0, 6.0, ((0, 128),)),
        "suffix_lengths": draw_suffix_lengths(jax.random.fold_in(splits[10], 71), 0),
        "prefix_of": draw_prefix_of(jax.random.fold_in(splits[10], 71), 0),
        "prefix_keys": draw_prefix_keys(jax.random.fold_in(splits[10], 71), 0),
        "prefix_values": bell_draw(splits[8], (PREFIXES, PLEN, KVH * HD), 1.0, 6.0, ((0, 16), (1, 8))),
        "prefix_lengths": draw_prefix_lengths(jax.random.fold_in(splits[10], 71), 0),
    }


def reference(queries, new_keys, new_values, suffix_keys, suffix_values, suffix_lengths, prefix_of, prefix_keys, prefix_values, prefix_lengths):
    group_size = H // KVH
    block_len = PLEN // N_REQ
    score_scale = HD ** -0.5

    def one_request(request_data):
        query_row, prefix_id, suffix_len, own_keys, own_values, fresh_keys, fresh_values = request_data
        query_f = query_row.astype(jnp.float32).reshape(STEPS, KVH, group_size, HD)
        pkeys = lax.dynamic_index_in_dim(prefix_keys, prefix_id, 0, keepdims=False)
        pvals = lax.dynamic_index_in_dim(prefix_values, prefix_id, 0, keepdims=False)
        pkeys = pkeys.astype(jnp.float32).reshape(N_REQ, block_len, KVH, HD)
        pvals = pvals.astype(jnp.float32).reshape(N_REQ, block_len, KVH, HD)
        prefix_len = prefix_lengths[prefix_id]
        scores = jnp.einsum("sghd,btgd->sghbt", query_f, pkeys) * score_scale
        valid_keys = (jnp.arange(PLEN, dtype=jnp.int32).reshape(N_REQ, block_len) < prefix_len)
        maxima = jnp.max(jnp.where(valid_keys, scores, -1e30), axis=-1)
        weights = jnp.where(valid_keys, jnp.exp(scores - maxima[..., None]), 0.0)
        totals = jnp.sum(weights, axis=-1)
        rounded = lax.optimization_barrier(weights.astype(jnp.bfloat16))
        outputs = jnp.einsum("sghbt,btgd->sghbd", rounded.astype(jnp.float32), pvals).astype(jnp.bfloat16)
        keys_all = jnp.concatenate([own_keys, fresh_keys], axis=0).astype(jnp.float32).reshape(SLEN + STEPS, KVH, HD)
        values_all = jnp.concatenate([own_values, fresh_values], axis=0).astype(jnp.float32).reshape(SLEN + STEPS, KVH, HD)
        own_scores = jnp.einsum("sghd,tgd->sght", query_f, keys_all) * score_scale
        places = jnp.arange(SLEN + STEPS, dtype=jnp.int32)
        step_ids = jnp.arange(STEPS, dtype=jnp.int32)
        own_valid = jnp.where(places[None, :] < SLEN, places[None, :] < suffix_len, (places[None, :] - SLEN) <= step_ids[:, None])
        own_valid = own_valid[:, None, None, :]
        own_max = jnp.max(jnp.where(own_valid, own_scores, -1e30), axis=-1)
        own_weights = jnp.where(own_valid, jnp.exp(own_scores - own_max[..., None]), 0.0)
        own_total = jnp.sum(own_weights, axis=-1)
        own_rounded = lax.optimization_barrier(own_weights.astype(jnp.bfloat16))
        own_out = jnp.einsum("sght,tgd->sghd", own_rounded.astype(jnp.float32), values_all)
        highest = jnp.maximum(own_max, jnp.max(maxima, axis=-1))
        block_scale = jnp.exp(maxima - highest[..., None])
        own_scale = jnp.exp(own_max - highest)
        numer = own_scale[..., None] * own_out + jnp.sum(block_scale[..., None] * outputs.astype(jnp.float32), axis=3)
        denom = own_scale * own_total + jnp.sum(block_scale * totals, axis=-1)
        return (numer / denom[..., None]).reshape(STEPS, H * HD).astype(jnp.bfloat16)

    batches = REQUESTS // 8

    def one_batch(request_batch):
        return jax.vmap(one_request)(request_batch)

    grouped = (
        queries.reshape(batches, 8, STEPS, H * HD),
        prefix_of.astype(jnp.int32).reshape(batches, 8),
        suffix_lengths.astype(jnp.int32).reshape(batches, 8),
        suffix_keys.reshape(batches, 8, SLEN, KVH * HD),
        suffix_values.reshape(batches, 8, SLEN, KVH * HD),
        new_keys.reshape(batches, 8, STEPS, KVH * HD),
        new_values.reshape(batches, 8, STEPS, KVH * HD),
    )
    attended = lax.map(one_batch, grouped)
    return attended.reshape(REQUESTS, STEPS, H * HD)
```

```python
import functools

import jax
import jax.numpy as jnp
from jax import lax
from jax.experimental import pallas as pl
from jax.experimental.pallas import tpu as pltpu
from jax.sharding import Mesh
from jax.sharding import PartitionSpec as P

F32 = jnp.float32
BF = jnp.bfloat16
HD = 128
CAP = 2
HEADS = 64
KVH = 4
STEPS = 2
GROUP = HEADS // KVH
ROWS = STEPS * GROUP
SCALE = HD ** -0.5
LOG2E = 1.4426950408889634
FACTOR = SCALE * LOG2E
EMPTY = 1024.0
LIMIT = 2.0 ** 100
LOW = -1e30
SLOTS = 16
TILE = 2048
TAIL = 512
SAMPLE = 256
VMEM_BYTES = 48 * 1024 * 1024


def dot_t(a, b):
    return lax.dot_general(a, b, (((1,), (1,)), ((), ())), preferred_element_type=F32)


def lane_sums(x):
    return sum(x[:, i * 128:(i + 1) * 128] for i in range(x.shape[1] // 128))


def pack_kernel(ids_ref, q_ref, out_ref, rank_ref, count):
    out_ref[...] = jnp.full(out_ref.shape, EMPTY, BF)
    for p in range(16):
        count[p] = 0
    for i in range(q_ref.shape[0]):
        p = ids_ref[i]
        j = count[p]
        count[p] = j + 1
        rank_ref[i] = j
        row = pl.multiple_of(j * ROWS, ROWS)
        for g in range(KVH):
            out_ref[p * KVH + g, pl.ds(row, ROWS), :] = q_ref[i, g]


def pack(ids, q4):
    smem = pl.BlockSpec(memory_space=pltpu.SMEM)
    vmem = pl.BlockSpec(memory_space=pltpu.VMEM)
    return pl.pallas_call(
        pack_kernel,
        out_shape=(
            jax.ShapeDtypeStruct((16 * KVH, CAP * ROWS, HD), BF),
            jax.ShapeDtypeStruct((16,), jnp.int32),
        ),
        in_specs=[smem, vmem],
        out_specs=(vmem, smem),
        scratch_shapes=[pltpu.SMEM((16,), jnp.int32)],
        name="pack",
    )(ids, q4)


def split_kernel(x_ref, k_ref, v_ref, o0, o1, o2, o3, sems):
    x = x_ref[0]
    copies = []
    for d, out in enumerate((o0, o1, o2, o3)):
        column = pl.multiple_of(lax.rem(x + d, 4) * HD, HD)
        for n, src in enumerate((k_ref, v_ref)):
            copy = pltpu.make_async_copy(
                src.at[:, pl.ds(column, HD)], out.at[n], sems.at[2 * d + n]
            )
            copy.start()
            copies.append(copy)
    for copy in copies:
        copy.wait()


def split_heads(x, keys, values):
    hbm = pl.BlockSpec(memory_space=pl.ANY)
    shape = jax.ShapeDtypeStruct((2, keys.shape[0], HD), BF)
    return pl.pallas_call(
        split_kernel,
        out_shape=(shape,) * 4,
        in_specs=[pl.BlockSpec(memory_space=pltpu.SMEM), hbm, hbm],
        out_specs=(hbm,) * 4,
        scratch_shapes=[pltpu.SemaphoreType.DMA((8,))],
        name="split_heads",
    )(x, keys, values)


def own_kernel(len_ref, q_ref, k_ref, v_ref, nk_ref, nv_ref, o_ref, st_ref):
    b = pl.program_id(0)
    per = q_ref.shape[0]
    lane = lax.broadcasted_iota(jnp.int32, (ROWS, 128), 1)
    row = lax.broadcasted_iota(jnp.int32, (ROWS, 128), 0)
    late = lax.broadcasted_iota(jnp.int32, (ROWS, 1), 0) >= GROUP
    col = lax.broadcasted_iota(jnp.int32, (ROWS, k_ref.shape[1]), 1)
    for i in range(per):
        live = col < len_ref[b * per + i]
        nk = nk_ref[i].astype(F32)
        nv = nv_ref[i].astype(F32)
        for g in range(KVH):
            part = slice(g * HD, (g + 1) * HD)
            q = q_ref[i, g]
            s = jnp.where(live, dot_t(q, k_ref[i, :, part]), LOW)
            qf = q.astype(F32)
            n0 = jnp.sum(qf * nk[0:1, part], axis=1, keepdims=True)
            n1 = jnp.sum(qf * nk[1:2, part], axis=1, keepdims=True)
            n1 = jnp.where(late, n1, LOW)
            top = jnp.maximum(jnp.max(s, axis=1, keepdims=True), jnp.maximum(n0, n1))
            shift = top * FACTOR
            w = jnp.exp2(s * FACTOR - shift)
            w0 = jnp.exp2(n0 * FACTOR - shift)
            w1 = jnp.exp2(n1 * FACTOR - shift)
            total = jnp.sum(w, axis=1, keepdims=True) + w0 + w1
            out = jnp.dot(w.astype(BF), v_ref[i, :, part], preferred_element_type=F32)
            out += w0.astype(BF).astype(F32) * nv[0:1, part]
            out += w1.astype(BF).astype(F32) * nv[1:2, part]
            o_ref[i, g] = out / total
            lse = top * SCALE + jnp.log(total)
            st_ref[i, g:g + 1, :] = jnp.sum(
                jnp.where(lane == row, lse, 0.0), axis=0, keepdims=True
            )


def own_attention(lengths, q4, keys, values, new_keys, new_values):
    n = q4.shape[0]
    per = 2
    span = keys.shape[1]
    wide = keys.shape[2]
    return pl.pallas_call(
        own_kernel,
        grid=(n // per,),
        out_shape=(
            jax.ShapeDtypeStruct((n, KVH, ROWS, HD), F32),
            jax.ShapeDtypeStruct((n, KVH, 128), F32),
        ),
        in_specs=[
            pl.BlockSpec(memory_space=pltpu.SMEM),
            pl.BlockSpec((per, KVH, ROWS, HD), lambda i: (i, 0, 0, 0)),
            pl.BlockSpec((per, span, wide), lambda i: (i, 0, 0)),
            pl.BlockSpec((per, span, wide), lambda i: (i, 0, 0)),
            pl.BlockSpec((per, STEPS, wide), lambda i: (i, 0, 0)),
            pl.BlockSpec((per, STEPS, wide), lambda i: (i, 0, 0)),
        ],
        out_specs=(
            pl.BlockSpec((per, KVH, ROWS, HD), lambda i: (i, 0, 0, 0)),
            pl.BlockSpec((per, KVH, 128), lambda i: (i, 0, 0)),
        ),
        compiler_params=pltpu.CompilerParams(vmem_limit_bytes=VMEM_BYTES),
        cost_estimate=pl.CostEstimate(
            flops=4 * n * HEADS * STEPS * span * HD, bytes_accessed=10 * 2**20, transcendentals=0
        ),
        name="own_attention",
    )(lengths, q4, keys, values, new_keys, new_values)


def flash_kernel(
    meta_ref, q_ref, a0, a1, a2, a3, b0, b1, b2, b3, out_ref,
    kbuf, vbuf, qc, oc, stc, st, acc, tot, mx, posv, poss, sems, psem,
):
    slots = q_ref.shape[0]
    length = meta_ref[0]
    x = meta_ref[1]
    core = meta_ref[2]
    block = a0.shape[1]
    copies = []
    for half, parts in enumerate(((a0, a1, a2, a3), (b0, b1, b2, b3))):
        side = core if half == 0 else 1 - core
        for d, part in enumerate(parts):
            start = pl.multiple_of((2 * lax.rem(x + d, 4) + side) * block, block)
            for n, buf in enumerate((kbuf, vbuf)):
                copy = pltpu.make_async_copy(
                    part.at[n], buf.at[pl.ds(start, block), :], sems.at[8 * half + 2 * d + n]
                )
                copy.start()
                copies.append(copy)
    lane16 = lax.broadcasted_iota(jnp.int32, (16, 128), 1)
    diag = jnp.zeros((16, 128), F32)
    for s in range(slots):
        diag = jnp.where(lane16 == s, q_ref[s, 0:16, :].astype(F32), diag)
    used = jnp.where(diag[0:1, :] < 0.5 * EMPTY, 1.0, 0.0)
    used = jnp.broadcast_to(used, (8, 128))
    r0 = lax.broadcasted_iota(jnp.int32, (128, 128), 0)
    r1 = lax.broadcasted_iota(jnp.int32, (128, 128), 1)
    upper = jnp.where(r0 < r1, 1.0, 0.0).astype(BF)
    before = jnp.dot(used.astype(BF), upper, preferred_element_type=F32)
    sub = lax.broadcasted_iota(jnp.int32, (8, 128), 0)
    posv[...] = jnp.where(sub == 0, before, before + used).astype(jnp.int32)
    copy = pltpu.make_async_copy(posv, poss, psem)
    copy.start()
    copy.wait()
    count = poss[1, 127]

    def gather(s, _):
        qc[pl.ds(pl.multiple_of(poss[0, s] * ROWS, ROWS), ROWS), :] = q_ref[s]
        return 0

    lax.fori_loop(0, slots, gather, 0, unroll=8)
    for copy in copies:
        copy.wait()
    rows = SLOTS * ROWS
    full = length // TILE
    rest = length - full * TILE
    tails = (rest + TAIL - 1) // TAIL

    def row_block(rb, _):
        row0 = pl.multiple_of(rb * rows, rows)
        span = pl.ds(row0, rows)

        def fixed(start, size, limit):
            s = dot_t(qc[span, :], kbuf[pl.ds(start, size), :])
            w = jnp.exp2(s * FACTOR - mx[...] * FACTOR)
            if limit is not None:
                col = lax.broadcasted_iota(jnp.int32, s.shape, 1)
                w = jnp.where(col < limit, w, 0.0)
            tot[...] += lane_sums(w)
            acc[...] += jnp.dot(
                w.astype(BF), vbuf[pl.ds(start, size), :], preferred_element_type=F32
            )

        def online(start, size, limit):
            s = dot_t(qc[span, :], kbuf[pl.ds(start, size), :])
            col = lax.broadcasted_iota(jnp.int32, s.shape, 1)
            s = jnp.where(col < limit, s, LOW)
            old = mx[...]
            new = jnp.maximum(old, jnp.max(s, axis=1, keepdims=True))
            w = jnp.exp2((s - new) * FACTOR)
            keep = jnp.exp2((old - new) * FACTOR)
            mx[...] = new
            tot[...] = tot[...] * keep + lane_sums(w)
            acc[...] = acc[...] * keep + jnp.dot(
                w.astype(BF), vbuf[pl.ds(start, size), :], preferred_element_type=F32
            )

        def fixed_tile(t, _):
            fixed(pl.multiple_of(t * TILE, TILE), TILE, None)
            return 0

        def fixed_tail(t, _):
            fixed(pl.multiple_of(full * TILE + t * TAIL, TAIL), TAIL, rest - t * TAIL)
            return 0

        def online_tile(t, _):
            online(pl.multiple_of(t * TAIL, TAIL), TAIL, length - t * TAIL)
            return 0

        sample = dot_t(qc[span, :], kbuf[0:SAMPLE, :])
        mx[...] = jnp.max(sample, axis=1, keepdims=True)
        tot[...] = jnp.zeros(tot.shape, F32)
        acc[...] = jnp.zeros(acc.shape, F32)
        lax.fori_loop(0, full, fixed_tile, 0)
        lax.fori_loop(0, tails, fixed_tail, 0)
        worst = jnp.max(jnp.where(tot[...] < LIMIT, 0.0, 1.0))

        @pl.when(worst > 0.0)
        def _():
            mx[...] = jnp.full(mx.shape, LOW, F32)
            tot[...] = jnp.zeros(tot.shape, F32)
            acc[...] = jnp.zeros(acc.shape, F32)
            lax.fori_loop(0, (length + TAIL - 1) // TAIL, online_tile, 0)

        total = jnp.sum(tot[...], axis=1, keepdims=True)
        oc[span, :] = (acc[...] / total).astype(BF)
        lse = mx[...] * SCALE + jnp.log(total)
        hi = lse.astype(BF).astype(F32)
        low = lse - hi
        mid = low.astype(BF).astype(F32)
        low = low - mid
        ln = lax.broadcasted_iota(jnp.int32, (rows, 128), 1)
        rw = lax.broadcasted_iota(jnp.int32, (rows, 128), 0)
        piece = jnp.where(ln < ROWS, hi, jnp.where(ln < 2 * ROWS, mid, low))
        piece = jnp.where((ln % ROWS == rw % ROWS) & (ln < 3 * ROWS), piece, 0.0)
        stc[pl.ds(pl.multiple_of(rb * SLOTS, SLOTS), SLOTS), :] = jnp.sum(
            piece.reshape(SLOTS, ROWS, 128), axis=1
        )
        return 0

    lax.fori_loop(0, (count + SLOTS - 1) // SLOTS, row_block, 0)

    def scatter(s, _):
        p = poss[0, s]
        out_ref[s // CAP, pl.ds(pl.multiple_of((s % CAP) * ROWS, ROWS), ROWS), :] = oc[
            pl.ds(pl.multiple_of(p * ROWS, ROWS), ROWS), :
        ]
        st[s // CAP, pl.ds(s % CAP, 1), :] = stc[pl.ds(p, 1), :]
        return 0

    lax.fori_loop(0, slots, scatter, 0, unroll=8)
    out_ref[:, CAP * ROWS:CAP * ROWS + 16, :] = st[...].astype(BF)


def prefix_attention(meta, q, parts):
    slots = q.shape[0]
    tokens = 8 * parts[0].shape[1]
    rows = SLOTS * ROWS
    hbm = pl.BlockSpec(memory_space=pl.ANY)
    vmem = pl.BlockSpec(memory_space=pltpu.VMEM)
    return pl.pallas_call(
        flash_kernel,
        out_shape=jax.ShapeDtypeStruct((slots // CAP, CAP * ROWS + 16, HD), BF),
        in_specs=[pl.BlockSpec(memory_space=pltpu.SMEM), vmem] + [hbm] * 8,
        out_specs=vmem,
        scratch_shapes=[
            pltpu.VMEM((tokens, HD), BF),
            pltpu.VMEM((tokens, HD), BF),
            pltpu.VMEM((slots * ROWS, HD), BF),
            pltpu.VMEM((slots * ROWS, HD), BF),
            pltpu.VMEM((slots, 128), F32),
            pltpu.VMEM((slots // CAP, 16, 128), F32),
            pltpu.VMEM((rows, HD), F32),
            pltpu.VMEM((rows, 128), F32),
            pltpu.VMEM((rows, 1), F32),
            pltpu.VMEM((8, 128), jnp.int32),
            pltpu.SMEM((8, 128), jnp.int32),
            pltpu.SemaphoreType.DMA((16,)),
            pltpu.SemaphoreType.DMA,
        ],
        compiler_params=pltpu.CompilerParams(vmem_limit_bytes=VMEM_BYTES),
        name="prefix_attention",
    )(meta, q, *parts)


def combine_kernel(ids_ref, rank_ref, ret_ref, own_ref, st_ref, out_ref):
    lane = lax.broadcasted_iota(jnp.int32, (ROWS, 128), 1)
    row = lax.broadcasted_iota(jnp.int32, (ROWS, 128), 0)
    pick = (lane % ROWS == row) & (lane < 3 * ROWS)
    same = lane == row
    sub = lax.broadcasted_iota(jnp.int32, (16, 128), 0)
    for i in range(own_ref.shape[0]):
        p = ids_ref[i]
        j = rank_ref[i]
        start = pl.multiple_of(j * ROWS, ROWS)
        for g in range(KVH):
            src = p * KVH + g
            stats = ret_ref[src, CAP * ROWS:CAP * ROWS + 16, :].astype(F32)
            stats = jnp.sum(jnp.where(sub == j, stats, 0.0), axis=0, keepdims=True)
            lse_p = jnp.sum(jnp.where(pick, stats, 0.0), axis=1, keepdims=True)
            lse_o = jnp.sum(jnp.where(same, st_ref[i, g:g + 1, :], 0.0), axis=1, keepdims=True)
            top = jnp.maximum(lse_p, lse_o)
            wp = jnp.exp(lse_p - top)
            wo = jnp.exp(lse_o - top)
            norm = 1.0 / (wp + wo)
            prefix = ret_ref[src, pl.ds(start, ROWS), :].astype(F32)
            out_ref[i, g] = (wp * norm * prefix + wo * norm * own_ref[i, g]).astype(BF)


def combine(ids, rank, ret, own, stats):
    smem = pl.BlockSpec(memory_space=pltpu.SMEM)
    vmem = pl.BlockSpec(memory_space=pltpu.VMEM)
    return pl.pallas_call(
        combine_kernel,
        out_shape=jax.ShapeDtypeStruct(own.shape, BF),
        in_specs=[smem, smem, vmem, vmem, vmem],
        out_specs=vmem,
        compiler_params=pltpu.CompilerParams(vmem_limit_bytes=VMEM_BYTES),
        name="combine",
    )(ids, rank, ret, own, stats)


def on_device(
    queries, new_keys, new_values, suffix_keys, suffix_values, suffix_lengths,
    prefix_of, prefix_keys, prefix_values, prefix_lengths,
):
    n = queries.shape[0]
    x = lax.axis_index("x").astype(jnp.int32)
    core = lax.axis_index("core").astype(jnp.int32)
    mine = split_heads(x.reshape(1), prefix_keys[0], prefix_values[0])
    parts = [mine[0]]
    for d in (1, 2, 3):
        moves = [(i, (i + d) % 4) for i in range(4)]
        parts.append(lax.ppermute(mine[d], "x", moves))
    parts = [parts[0], parts[3], parts[2], parts[1]]
    other = [lax.ppermute(part, "core", [(0, 1), (1, 0)]) for part in parts]

    q4 = queries.reshape(n, STEPS, KVH, GROUP, HD).transpose(0, 2, 1, 3, 4)
    q4 = q4.reshape(n, KVH, ROWS, HD)
    send, rank = pack(prefix_of, q4)
    arrived = lax.all_to_all(send, ("prefix", "x"), split_axis=0, concat_axis=0, tiled=True)
    own, stats = own_attention(
        suffix_lengths, q4, suffix_keys, suffix_values, new_keys, new_values
    )
    meta = jnp.stack([prefix_lengths[0], x, core])
    back = prefix_attention(
        meta, arrived.reshape(arrived.shape[0] * CAP, ROWS, HD), parts + other
    )
    ret = lax.all_to_all(back, ("prefix", "x"), split_axis=0, concat_axis=0, tiled=True)
    out = combine(prefix_of, rank, ret, own, stats)
    out = out.reshape(n, KVH, STEPS, GROUP, HD).transpose(0, 2, 1, 3, 4)
    return out.reshape(n, STEPS, HEADS * HD)


def solution(mesh):
    split = Mesh(mesh.devices.reshape(mesh.devices.shape[0], -1, 2), ("prefix", "x", "core"))
    every = ("prefix", "x", "core")
    row = ("x", "core")
    placed = (
        P(every, None, None),
        P(every, None, None),
        P(every, None, None),
        P(every, None, None),
        P(every, None, None),
        P(every),
        P(every),
        P("prefix", row, None),
        P("prefix", row, None),
        P("prefix"),
    )
    return jax.shard_map(
        on_device,
        mesh=split,
        in_specs=placed,
        out_specs=P(every, None, None),
        check_vma=False,
    )
```

```python
import functools

import jax
import jax.numpy as jnp
from jax import lax
from jax.experimental import pallas as pl
from jax.experimental.pallas import tpu as pltpu
from jax.sharding import Mesh
from jax.sharding import PartitionSpec as P

F32 = jnp.float32
BF = jnp.bfloat16
HD = 128
CAP = 2
HEADS = 64
KVH = 4
STEPS = 2
GROUP = HEADS // KVH
ROWS = STEPS * GROUP
SCALE = HD ** -0.5
LOG2E = 1.4426950408889634
FACTOR = SCALE * LOG2E
EMPTY = 1024.0
LIMIT = 2.0 ** 100
LOW = -1e30
SLOTS = 16
TILE = 2048
TAIL = 512
SAMPLE = 256
VMEM_BYTES = 48 * 1024 * 1024


def dot_t(a, b):
    return lax.dot_general(a, b, (((1,), (1,)), ((), ())), preferred_element_type=F32)


def lane_sums(x):
    return sum(x[:, i * 128:(i + 1) * 128] for i in range(x.shape[1] // 128))


def route_kernel(x_ref, ids_ref, q_ref, o1, o2, o3, rank_ref, slot_ref, count):
    x = x_ref[0]
    n = q_ref.shape[1]
    for p in range(16):
        count[p] = 0
    lane = lax.broadcasted_iota(jnp.int32, (16, 128), 1)
    names = jnp.zeros((16, 128), jnp.int32)
    for i in range(n):
        p = ids_ref[i]
        j = count[p]
        count[p] = j + 1
        rank_ref[i] = j
        slot_ref[i] = p * CAP + j
        names = jnp.where(lane == i, p * CAP + j, names)
    names = names.astype(F32).astype(BF)
    for d, out in enumerate((o1, o2, o3)):
        out[0:n * ROWS, :] = q_ref[lax.rem(x + d + 1, 4)].reshape(n * ROWS, HD)
        out[n * ROWS:n * ROWS + 16, :] = names


def route(x, ids, qg):
    smem = pl.BlockSpec(memory_space=pltpu.SMEM)
    vmem = pl.BlockSpec(memory_space=pltpu.VMEM)
    n = qg.shape[1]
    part = jax.ShapeDtypeStruct((n * ROWS + 16, HD), BF)
    index = jax.ShapeDtypeStruct((n,), jnp.int32)
    return pl.pallas_call(
        route_kernel,
        out_shape=(part, part, part, index, index),
        in_specs=[smem, smem, vmem],
        out_specs=(vmem, vmem, vmem, smem, smem),
        scratch_shapes=[pltpu.SMEM((16,), jnp.int32)],
        name="route",
    )(x, ids, qg)


def pack_kernel(x_ref, slot_ref, q_ref, p1, p2, p3, out_ref, names, slots, sem):
    x = x_ref[0]
    n = q_ref.shape[1]
    for d, part in enumerate((p1, p2, p3)):
        names[d * 16:d * 16 + 16, :] = part[n * ROWS:n * ROWS + 16, :].astype(F32).astype(jnp.int32)
    copy = pltpu.make_async_copy(names, slots, sem)
    copy.start()
    out_ref[...] = jnp.full(out_ref.shape, EMPTY, BF)

    def place(source, slot, rows):
        start = pl.multiple_of(lax.rem(slot, CAP) * ROWS, ROWS)
        out_ref[slot // CAP, source, pl.ds(start, ROWS), :] = rows

    for i in range(n):
        place(x, slot_ref[i], q_ref[x, i])
    copy.wait()
    for d, part in enumerate((p1, p2, p3)):
        source = lax.rem(x + d + 1, 4)
        for i in range(n):
            place(source, slots[d * 16, i], part[i * ROWS:(i + 1) * ROWS, :])


def pack(x, slot, qg, parts):
    smem = pl.BlockSpec(memory_space=pltpu.SMEM)
    vmem = pl.BlockSpec(memory_space=pltpu.VMEM)
    return pl.pallas_call(
        pack_kernel,
        out_shape=jax.ShapeDtypeStruct((16, 4, CAP * ROWS, HD), BF),
        in_specs=[smem, smem, vmem, vmem, vmem, vmem],
        out_specs=vmem,
        scratch_shapes=[
            pltpu.VMEM((48, 128), jnp.int32),
            pltpu.SMEM((48, 128), jnp.int32),
            pltpu.SemaphoreType.DMA,
        ],
        name="pack",
    )(x, slot, qg, *parts)


def split_kernel(x_ref, k_ref, v_ref, o0, o1, o2, o3, vbuf, sems):
    x = x_ref[0]
    copies = []
    for d, out in enumerate((o0, o1, o2, o3)):
        column = pl.multiple_of(lax.rem(x + d, 4) * HD, HD)
        copy_k = pltpu.make_async_copy(k_ref.at[:, pl.ds(column, HD)], out.at[0], sems.at[2 * d])
        copy_v = pltpu.make_async_copy(v_ref.at[:, pl.ds(column, HD)], vbuf.at[d], sems.at[2 * d + 1])
        copy_v.start()
        copy_k.start()
        copies.append((copy_k, copy_v))
    for d, out in enumerate((o0, o1, o2, o3)):
        copies[d][1].wait()
        for b in range(vbuf.shape[1] // HD):
            part = slice(b * HD, (b + 1) * HD)
            out[1, part, :] = vbuf[d, part, :].T
    for copy_k, _ in copies:
        copy_k.wait()


def split_heads(x, keys, values):
    hbm = pl.BlockSpec(memory_space=pl.ANY)
    vmem = pl.BlockSpec(memory_space=pltpu.VMEM)
    tokens = keys.shape[0]
    shape = jax.ShapeDtypeStruct((2, tokens, HD), BF)
    return pl.pallas_call(
        split_kernel,
        out_shape=(shape,) * 4,
        in_specs=[pl.BlockSpec(memory_space=pltpu.SMEM), hbm, hbm],
        out_specs=(vmem,) * 4,
        scratch_shapes=[pltpu.VMEM((4, tokens, HD), BF), pltpu.SemaphoreType.DMA((8,))],
        name="split_heads",
    )(x, keys, values)


def own_kernel(len_ref, q_ref, k_ref, v_ref, nk_ref, nv_ref, o_ref, st_ref):
    b = pl.program_id(0)
    per = q_ref.shape[1]
    lane = lax.broadcasted_iota(jnp.int32, (ROWS, 128), 1)
    row = lax.broadcasted_iota(jnp.int32, (ROWS, 128), 0)
    late = lax.broadcasted_iota(jnp.int32, (ROWS, 1), 0) >= GROUP
    col = lax.broadcasted_iota(jnp.int32, (ROWS, k_ref.shape[1]), 1)
    for i in range(per):
        live = col < len_ref[b * per + i]
        nk = nk_ref[i].astype(F32)
        nv = nv_ref[i].astype(F32)
        for g in range(KVH):
            part = slice(g * HD, (g + 1) * HD)
            q = q_ref[g, i]
            s = jnp.where(live, dot_t(q, k_ref[i, :, part]), LOW)
            qf = q.astype(F32)
            n0 = jnp.sum(qf * nk[0:1, part], axis=1, keepdims=True)
            n1 = jnp.sum(qf * nk[1:2, part], axis=1, keepdims=True)
            n1 = jnp.where(late, n1, LOW)
            top = jnp.maximum(jnp.max(s, axis=1, keepdims=True), jnp.maximum(n0, n1))
            shift = top * FACTOR
            w = jnp.exp2(s * FACTOR - shift)
            w0 = jnp.exp2(n0 * FACTOR - shift)
            w1 = jnp.exp2(n1 * FACTOR - shift)
            total = jnp.sum(w, axis=1, keepdims=True) + w0 + w1
            out = jnp.dot(w.astype(BF), v_ref[i, :, part], preferred_element_type=F32)
            out += w0.astype(BF).astype(F32) * nv[0:1, part]
            out += w1.astype(BF).astype(F32) * nv[1:2, part]
            o_ref[i, g] = out / total
            lse = top * SCALE + jnp.log(total)
            st_ref[i, g:g + 1, :] = jnp.sum(
                jnp.where(lane == row, lse, 0.0), axis=0, keepdims=True
            )


def own_attention(lengths, qg, keys, values, new_keys, new_values):
    n = qg.shape[1]
    per = 2
    span = keys.shape[1]
    wide = keys.shape[2]
    return pl.pallas_call(
        own_kernel,
        grid=(n // per,),
        out_shape=(
            jax.ShapeDtypeStruct((n, KVH, ROWS, HD), F32),
            jax.ShapeDtypeStruct((n, KVH, 128), F32),
        ),
        in_specs=[
            pl.BlockSpec(memory_space=pltpu.SMEM),
            pl.BlockSpec((KVH, per, ROWS, HD), lambda i: (0, i, 0, 0)),
            pl.BlockSpec((per, span, wide), lambda i: (i, 0, 0)),
            pl.BlockSpec((per, span, wide), lambda i: (i, 0, 0)),
            pl.BlockSpec((per, STEPS, wide), lambda i: (i, 0, 0)),
            pl.BlockSpec((per, STEPS, wide), lambda i: (i, 0, 0)),
        ],
        out_specs=(
            pl.BlockSpec((per, KVH, ROWS, HD), lambda i: (i, 0, 0, 0)),
            pl.BlockSpec((per, KVH, 128), lambda i: (i, 0, 0)),
        ),
        compiler_params=pltpu.CompilerParams(vmem_limit_bytes=VMEM_BYTES),
        cost_estimate=pl.CostEstimate(
            flops=4 * n * HEADS * STEPS * span * HD, bytes_accessed=10 * 2**20, transcendentals=0
        ),
        name="own_attention",
    )(lengths, qg, keys, values, new_keys, new_values)


def flash_kernel(
    meta_ref, q_ref, a0, a1, a2, a3, b0, b1, b2, b3, out_ref,
    kbuf, vbuf, qc, oc, stc, st, acc, tot, mx, bad, pick, posv, poss, sems, psem,
):
    slots = q_ref.shape[0]
    rows = SLOTS * ROWS
    length = meta_ref[0]
    x = meta_ref[1]
    core = meta_ref[2]
    block = a0.shape[1]
    for half, parts in enumerate(((a0, a1, a2, a3), (b0, b1, b2, b3))):
        side = core if half == 0 else 1 - core
        for d, part in enumerate(parts):
            start = pl.multiple_of((2 * lax.rem(x + d, 4) + side) * block, block)
            pltpu.make_async_copy(part.at[0], kbuf.at[pl.ds(start, block), :], sems.at[0]).start()
            for b in range(block // HD):
                pltpu.make_async_copy(
                    part.at[1, pl.ds(b * HD, HD), :],
                    vbuf.at[:, pl.ds(pl.multiple_of(start + b * HD, HD), HD)],
                    sems.at[1],
                ).start()

    lane16 = lax.broadcasted_iota(jnp.int32, (16, 128), 1)
    diag = jnp.zeros((16, 128), F32)
    for s in range(slots):
        diag = jnp.where(lane16 == s, q_ref[s, 0:16, :].astype(F32), diag)
    used = jnp.where(diag[0:1, :] < 0.5 * EMPTY, 1.0, 0.0)
    used = jnp.broadcast_to(used, (8, 128))
    r0 = lax.broadcasted_iota(jnp.int32, (128, 128), 0)
    r1 = lax.broadcasted_iota(jnp.int32, (128, 128), 1)
    upper = jnp.where(r0 < r1, 1.0, 0.0).astype(BF)
    before = jnp.dot(used.astype(BF), upper, preferred_element_type=F32)
    sub = lax.broadcasted_iota(jnp.int32, (8, 128), 0)
    posv[...] = jnp.where(sub == 0, before, before + used).astype(jnp.int32)
    copy = pltpu.make_async_copy(posv, poss, psem)
    copy.start()
    p0 = lax.broadcasted_iota(jnp.int32, (3 * rows, 128), 0)
    p1 = lax.broadcasted_iota(jnp.int32, (3 * rows, 128), 1)
    pick[...] = jnp.where(p1 == p0 // rows * ROWS + p0 % ROWS, 1.0, 0.0).astype(BF)
    bad[...] = jnp.zeros(bad.shape, F32)
    copy.wait()
    count = poss[1, 127]

    def gather(s, _):
        qc[pl.ds(pl.multiple_of(poss[0, s] * ROWS, ROWS), ROWS), :] = q_ref[s]
        return 0

    lax.fori_loop(0, slots, gather, 0, unroll=8)
    qc[pl.ds(pl.multiple_of(count * ROWS, ROWS), rows), :] = jnp.zeros((rows, HD), BF)
    pltpu.make_async_copy(kbuf, kbuf, sems.at[0]).wait()
    pltpu.make_async_copy(vbuf, vbuf, sems.at[1]).wait()
    blocks = (count + SLOTS - 1) // SLOTS
    full = length // TILE
    rest = length - full * TILE
    half_tile = rest // (TILE // 2)
    rest = rest - half_tile * (TILE // 2)
    tails = (rest + TAIL - 1) // TAIL

    def shift_block(rb, _):
        q = qc[pl.ds(pl.multiple_of(rb * rows, rows), rows), :]
        mx[rb] = jnp.max(dot_t(kbuf[0:SAMPLE, :], q), axis=0, keepdims=True)
        return 0

    lax.fori_loop(0, blocks, shift_block, 0)

    def finish(rb):
        span = pl.ds(pl.multiple_of(rb * rows, rows), rows)
        total = jnp.sum(tot[...], axis=0, keepdims=True)
        bad[...] = jnp.maximum(bad[...], jnp.where(total < LIMIT, 0.0, 1.0))
        oc[span, :] = (acc[...] / total).T.astype(BF)
        lse = mx[rb] * SCALE + jnp.log(total)
        hi = lse.astype(BF)
        low = lse - hi.astype(F32)
        mid = low.astype(BF)
        low = (low - mid.astype(F32)).astype(BF)
        flat = jnp.concatenate([hi, mid, low], axis=1)
        sl = lax.broadcasted_iota(jnp.int32, (SLOTS, 3 * rows), 0)
        ln = lax.broadcasted_iota(jnp.int32, (SLOTS, 3 * rows), 1)
        spread = jnp.where(ln % rows // ROWS == sl, flat.astype(F32), 0.0).astype(BF)
        stc[pl.ds(pl.multiple_of(rb * SLOTS, SLOTS), SLOTS), :] = jnp.dot(
            spread, pick[...], preferred_element_type=F32
        )

    def row_block(rb, _):
        span = pl.ds(pl.multiple_of(rb * rows, rows), rows)

        def fixed(start, size, limit):
            s = dot_t(kbuf[pl.ds(start, size), :], qc[span, :])
            w = jnp.exp2(s * FACTOR - mx[rb] * FACTOR)
            if limit is not None:
                token = lax.broadcasted_iota(jnp.int32, s.shape, 0)
                w = jnp.where(token < limit, w, 0.0)
            tot[...] += jnp.sum(w.reshape(size // 8, 8, rows), axis=0)
            acc[...] += jnp.dot(
                vbuf[:, pl.ds(start, size)], w.astype(BF), preferred_element_type=F32
            )

        def fixed_tile(t, _):
            fixed(pl.multiple_of(t * TILE, TILE), TILE, None)
            return 0

        def fixed_half(t, _):
            fixed(pl.multiple_of(full * TILE, TILE), TILE // 2, None)
            return 0

        def fixed_tail(t, _):
            start = full * TILE + half_tile * (TILE // 2) + t * TAIL
            fixed(pl.multiple_of(start, TAIL), TAIL, rest - t * TAIL)
            return 0

        tot[...] = jnp.zeros(tot.shape, F32)
        acc[...] = jnp.zeros(acc.shape, F32)
        lax.fori_loop(0, full, fixed_tile, 0)
        lax.fori_loop(0, half_tile, fixed_half, 0)
        lax.fori_loop(0, tails, fixed_tail, 0)
        finish(rb)
        return 0

    def careful_block(rb, _):
        span = pl.ds(pl.multiple_of(rb * rows, rows), rows)

        def online(t, _):
            start = pl.multiple_of(t * TAIL, TAIL)
            s = dot_t(kbuf[pl.ds(start, TAIL), :], qc[span, :])
            token = lax.broadcasted_iota(jnp.int32, s.shape, 0)
            s = jnp.where(token < length - start, s, LOW)
            old = mx[rb]
            new = jnp.maximum(old, jnp.max(s, axis=0, keepdims=True))
            w = jnp.exp2((s - new) * FACTOR)
            keep = jnp.exp2((old - new) * FACTOR)
            mx[rb] = new
            tot[...] = tot[...] * keep + jnp.sum(w.reshape(TAIL // 8, 8, rows), axis=0)
            acc[...] = acc[...] * keep + jnp.dot(
                vbuf[:, pl.ds(start, TAIL)], w.astype(BF), preferred_element_type=F32
            )
            return 0

        mx[rb] = jnp.full((1, rows), LOW, F32)
        tot[...] = jnp.zeros(tot.shape, F32)
        acc[...] = jnp.zeros(acc.shape, F32)
        lax.fori_loop(0, (length + TAIL - 1) // TAIL, online, 0)
        finish(rb)
        return 0

    lax.fori_loop(0, blocks, row_block, 0)

    @pl.when(jnp.max(bad[...]) > 0.0)
    def _():
        lax.fori_loop(0, blocks, careful_block, 0)

    def scatter(s, _):
        p = poss[0, s]
        out_ref[s // CAP, pl.ds(pl.multiple_of((s % CAP) * ROWS, ROWS), ROWS), :] = oc[
            pl.ds(pl.multiple_of(p * ROWS, ROWS), ROWS), :
        ]
        st[s // CAP, pl.ds(s % CAP, 1), :] = stc[pl.ds(p, 1), :]
        return 0

    lax.fori_loop(0, slots, scatter, 0, unroll=8)
    out_ref[:, CAP * ROWS:CAP * ROWS + 16, :] = st[...].astype(BF)


def prefix_attention(meta, q, parts):
    slots = q.shape[0]
    tokens = 8 * parts[0].shape[1]
    rows = SLOTS * ROWS
    hbm = pl.BlockSpec(memory_space=pl.ANY)
    vmem = pl.BlockSpec(memory_space=pltpu.VMEM)
    return pl.pallas_call(
        flash_kernel,
        out_shape=jax.ShapeDtypeStruct((slots // CAP, CAP * ROWS + 16, HD), BF),
        in_specs=[pl.BlockSpec(memory_space=pltpu.SMEM), vmem] + [hbm] * 8,
        out_specs=vmem,
        scratch_shapes=[
            pltpu.VMEM((tokens, HD), BF),
            pltpu.VMEM((HD, tokens), BF),
            pltpu.VMEM((slots * ROWS + rows, HD), BF),
            pltpu.VMEM((slots * ROWS, HD), BF),
            pltpu.VMEM((slots, 128), F32),
            pltpu.VMEM((slots // CAP, 16, 128), F32),
            pltpu.VMEM((HD, rows), F32),
            pltpu.VMEM((8, rows), F32),
            pltpu.VMEM((slots // SLOTS, 1, rows), F32),
            pltpu.VMEM((1, rows), F32),
            pltpu.VMEM((3 * rows, 128), BF),
            pltpu.VMEM((8, 128), jnp.int32),
            pltpu.SMEM((8, 128), jnp.int32),
            pltpu.SemaphoreType.DMA((2,)),
            pltpu.SemaphoreType.DMA,
        ],
        compiler_params=pltpu.CompilerParams(vmem_limit_bytes=VMEM_BYTES),
        name="prefix_attention",
    )(meta, q, *parts)


def combine_kernel(ids_ref, rank_ref, ret_ref, own_ref, st_ref, out_ref):
    lane = lax.broadcasted_iota(jnp.int32, (ROWS, 128), 1)
    row = lax.broadcasted_iota(jnp.int32, (ROWS, 128), 0)
    pick = (lane % ROWS == row) & (lane < 3 * ROWS)
    same = lane == row
    sub = lax.broadcasted_iota(jnp.int32, (16, 128), 0)
    for i in range(own_ref.shape[0]):
        p = ids_ref[i]
        j = rank_ref[i]
        start = pl.multiple_of(j * ROWS, ROWS)
        for g in range(KVH):
            src = p * KVH + g
            stats = ret_ref[src, CAP * ROWS:CAP * ROWS + 16, :].astype(F32)
            stats = jnp.sum(jnp.where(sub == j, stats, 0.0), axis=0, keepdims=True)
            lse_p = jnp.sum(jnp.where(pick, stats, 0.0), axis=1, keepdims=True)
            lse_o = jnp.sum(jnp.where(same, st_ref[i, g:g + 1, :], 0.0), axis=1, keepdims=True)
            top = jnp.maximum(lse_p, lse_o)
            wp = jnp.exp(lse_p - top)
            wo = jnp.exp(lse_o - top)
            norm = 1.0 / (wp + wo)
            prefix = ret_ref[src, pl.ds(start, ROWS), :].astype(F32)
            out_ref[i, g] = (wp * norm * prefix + wo * norm * own_ref[i, g]).astype(BF)


def combine(ids, rank, ret, own, stats):
    smem = pl.BlockSpec(memory_space=pltpu.SMEM)
    vmem = pl.BlockSpec(memory_space=pltpu.VMEM)
    return pl.pallas_call(
        combine_kernel,
        out_shape=jax.ShapeDtypeStruct(own.shape, BF),
        in_specs=[smem, smem, vmem, vmem, vmem],
        out_specs=vmem,
        compiler_params=pltpu.CompilerParams(vmem_limit_bytes=VMEM_BYTES),
        name="combine",
    )(ids, rank, ret, own, stats)


def on_device(
    queries, new_keys, new_values, suffix_keys, suffix_values, suffix_lengths,
    prefix_of, prefix_keys, prefix_values, prefix_lengths,
):
    n = queries.shape[0]
    x = lax.axis_index("x").astype(jnp.int32)
    core = lax.axis_index("core").astype(jnp.int32)
    moves = {d: [(i, (i + d) % 4) for i in range(4)] for d in (1, 2, 3)}
    qg = queries.reshape(n, STEPS, KVH, GROUP, HD).transpose(2, 0, 1, 3, 4)
    qg = qg.reshape(KVH, n, ROWS, HD)
    r1, r2, r3, rank, slot = route(x.reshape(1), prefix_of, qg)
    q3 = lax.ppermute(r1, "x", moves[1])
    q1 = lax.ppermute(r3, "x", moves[3])
    q2 = lax.ppermute(r2, "x", moves[2])
    mine = split_heads(x.reshape(1), prefix_keys[0], prefix_values[0])
    parts = [mine[0]] + [lax.ppermute(mine[4 - d], "x", moves[4 - d]) for d in (1, 2, 3)]
    other = [lax.ppermute(part, "core", [(0, 1), (1, 0)]) for part in parts]
    send = pack(x.reshape(1), slot, qg, (q1, q2, q3))
    arrived = lax.all_to_all(send, "prefix", split_axis=0, concat_axis=0, tiled=True)
    own, stats = own_attention(
        suffix_lengths, qg, suffix_keys, suffix_values, new_keys, new_values
    )
    meta = jnp.stack([prefix_lengths[0], x, core])
    back = prefix_attention(
        meta, arrived.reshape(-1, ROWS, HD), parts + other
    )
    ret = lax.all_to_all(back, ("prefix", "x"), split_axis=0, concat_axis=0, tiled=True)
    out = combine(prefix_of, rank, ret, own, stats)
    out = out.reshape(n, KVH, STEPS, GROUP, HD).transpose(0, 2, 1, 3, 4)
    return out.reshape(n, STEPS, HEADS * HD)


def solution(mesh):
    split = Mesh(mesh.devices.reshape(mesh.devices.shape[0], -1, 2), ("prefix", "x", "core"))
    every = ("prefix", "x", "core")
    row = ("x", "core")
    placed = (
        P(every, None, None),
        P(every, None, None),
        P(every, None, None),
        P(every, None, None),
        P(every, None, None),
        P(every),
        P(every),
        P("prefix", row, None),
        P("prefix", row, None),
        P("prefix"),
    )
    return jax.shard_map(
        on_device,
        mesh=split,
        in_specs=placed,
        out_specs=P(every, None, None),
        check_vma=False,
    )
```

```python
import functools

import jax
import jax.numpy as jnp
from jax import lax
from jax.experimental import pallas as pl
from jax.experimental.pallas import tpu as pltpu
from jax.sharding import Mesh
from jax.sharding import PartitionSpec as P

F32 = jnp.float32
BF = jnp.bfloat16
HD = 128
CAP = 2
HEADS = 64
KVH = 4
STEPS = 2
GROUP = HEADS // KVH
ROWS = STEPS * GROUP
SCALE = HD ** -0.5
LOG2E = 1.4426950408889634
FACTOR = SCALE * LOG2E
EMPTY = 1024.0
LIMIT = 2.0 ** 100
LOW = -1e30
SLOTS = 16
STATS = 8
TILE = 2048
TAIL = 512
SAMPLE = 256
SMALL_VMEM = 14 * 1024 * 1024
VMEM_BYTES = 32 * 1024 * 1024


def dot_t(a, b):
    return lax.dot_general(a, b, (((1,), (1,)), ((), ())), preferred_element_type=F32)


def lane_sums(x):
    return sum(x[:, i * 128:(i + 1) * 128] for i in range(x.shape[1] // 128))


def route_kernel(x_ref, ids_ref, q_ref, o1, o2, o3, rank_ref, slot_ref, count, sems):
    x = x_ref[0]
    n = q_ref.shape[0]
    copies = []
    for d, out in enumerate((o1, o2, o3)):
        copy = pltpu.make_async_copy(
            q_ref.at[:, lax.rem(x + d + 1, 4)], out.at[0:n], sems.at[d]
        )
        copy.start()
        copies.append(copy)
    for p in range(16):
        count[p] = 0
    lane = lax.broadcasted_iota(jnp.int32, (ROWS, 128), 1)
    names = jnp.zeros((ROWS, 128), jnp.int32)
    for i in range(n):
        p = ids_ref[i]
        j = count[p]
        count[p] = j + 1
        rank_ref[i] = j
        slot_ref[i] = p * CAP + j
        names = jnp.where(lane == i, p * CAP + j, names)
    names = names.astype(F32).astype(BF)
    for out in (o1, o2, o3):
        out[n] = names
    for copy in copies:
        copy.wait()


def route(x, ids, q4):
    smem = pl.BlockSpec(memory_space=pltpu.SMEM)
    vmem = pl.BlockSpec(memory_space=pltpu.VMEM)
    n = q4.shape[0]
    part = jax.ShapeDtypeStruct((n + 1, ROWS, HD), BF)
    index = jax.ShapeDtypeStruct((n,), jnp.int32)
    return pl.pallas_call(
        route_kernel,
        out_shape=(part, part, part, index, index),
        in_specs=[smem, smem, pl.BlockSpec(memory_space=pl.ANY)],
        out_specs=(vmem, vmem, vmem, smem, smem),
        scratch_shapes=[pltpu.SMEM((16,), jnp.int32), pltpu.SemaphoreType.DMA((3,))],
        compiler_params=pltpu.CompilerParams(vmem_limit_bytes=SMALL_VMEM),
        name="route",
    )(x, ids, q4)


def pack_kernel(x_ref, slot_ref, q_ref, p1, p2, p3, out_ref, mine, names, slots, sems):
    x = x_ref[0]
    n = q_ref.shape[0]
    copy_q = pltpu.make_async_copy(q_ref.at[:, x], mine, sems.at[0])
    copy_q.start()
    for d, part in enumerate((p1, p2, p3)):
        names[d * 16:d * 16 + 16, :] = part[n, 0:16, :].astype(F32).astype(jnp.int32)
    copy = pltpu.make_async_copy(names, slots, sems.at[1])
    copy.start()
    out_ref[...] = jnp.full(out_ref.shape, EMPTY, BF)

    def place(source, slot, rows):
        start = pl.multiple_of(lax.rem(slot, CAP) * ROWS, ROWS)
        out_ref[slot // CAP, source, pl.ds(start, ROWS), :] = rows

    copy_q.wait()
    for i in range(n):
        place(x, slot_ref[i], mine[i])
    copy.wait()
    for d, part in enumerate((p1, p2, p3)):
        source = lax.rem(x + d + 1, 4)
        for i in range(n):
            place(source, slots[d * 16, i], part[i])


def pack(x, slot, q4, parts):
    smem = pl.BlockSpec(memory_space=pltpu.SMEM)
    vmem = pl.BlockSpec(memory_space=pltpu.VMEM)
    return pl.pallas_call(
        pack_kernel,
        out_shape=jax.ShapeDtypeStruct((16, 4, CAP * ROWS, HD), BF),
        in_specs=[smem, smem, pl.BlockSpec(memory_space=pl.ANY), vmem, vmem, vmem],
        out_specs=vmem,
        scratch_shapes=[
            pltpu.VMEM((q4.shape[0], ROWS, HD), BF),
            pltpu.VMEM((48, 128), jnp.int32),
            pltpu.SMEM((48, 128), jnp.int32),
            pltpu.SemaphoreType.DMA((2,)),
        ],
        compiler_params=pltpu.CompilerParams(vmem_limit_bytes=SMALL_VMEM),
        name="pack",
    )(x, slot, q4, *parts)


def split_kernel(x_ref, k_ref, v_ref, o0, o1, o2, o3, vbuf, sems):
    x = x_ref[0]
    copies = []
    for d, out in enumerate((o0, o1, o2, o3)):
        column = pl.multiple_of(lax.rem(x + d, 4) * HD, HD)
        copy_k = pltpu.make_async_copy(k_ref.at[:, pl.ds(column, HD)], out.at[0], sems.at[2 * d])
        copy_v = pltpu.make_async_copy(v_ref.at[:, pl.ds(column, HD)], vbuf.at[d], sems.at[2 * d + 1])
        copy_v.start()
        copy_k.start()
        copies.append((copy_k, copy_v))
    for d, out in enumerate((o0, o1, o2, o3)):
        copies[d][1].wait()
        for b in range(vbuf.shape[1] // HD):
            part = slice(b * HD, (b + 1) * HD)
            out[1, part, :] = vbuf[d, part, :].T
    for copy_k, _ in copies:
        copy_k.wait()


def split_heads(x, keys, values):
    hbm = pl.BlockSpec(memory_space=pl.ANY)
    vmem = pl.BlockSpec(memory_space=pltpu.VMEM)
    tokens = keys.shape[0]
    shape = jax.ShapeDtypeStruct((2, tokens, HD), BF)
    return pl.pallas_call(
        split_kernel,
        out_shape=(shape,) * 4,
        in_specs=[pl.BlockSpec(memory_space=pltpu.SMEM), hbm, hbm],
        out_specs=(vmem,) * 4,
        scratch_shapes=[pltpu.VMEM((4, tokens, HD), BF), pltpu.SemaphoreType.DMA((8,))],
        compiler_params=pltpu.CompilerParams(vmem_limit_bytes=SMALL_VMEM),
        name="split_heads",
    )(x, keys, values)


def own_kernel(len_ref, q_ref, k_ref, v_ref, nk_ref, nv_ref, o_ref, st_ref, *, first):
    per = q_ref.shape[0]
    base = first + pl.program_id(0) * per
    pairs = [(i, g) for i in range(per) for g in range(KVH)]
    rows = len(pairs) * ROWS

    def part(g):
        return slice(g * HD, (g + 1) * HD)

    def spread(ref, step):
        return jnp.concatenate(
            [
                jnp.broadcast_to(ref[i, step:step + 1, part(g)].astype(F32), (ROWS, HD))
                for i, g in pairs
            ],
            axis=0,
        )

    s = jnp.concatenate([dot_t(q_ref[i, g], k_ref[i, :, part(g)]) for i, g in pairs], axis=0)
    row = lax.broadcasted_iota(jnp.int32, (rows, 1), 0)
    late = row % STEPS >= 1
    limit = jnp.full((rows, 1), len_ref[base], jnp.int32)
    for i in range(1, per):
        limit = jnp.where(row >= i * KVH * ROWS, len_ref[base + i], limit)
    col = lax.broadcasted_iota(jnp.int32, s.shape, 1)
    s = jnp.where(col < limit, s, LOW)
    q = jnp.concatenate([q_ref[i, g] for i, g in pairs], axis=0).astype(F32)
    n0 = jnp.sum(q * spread(nk_ref, 0), axis=1, keepdims=True)
    n1 = jnp.where(late, jnp.sum(q * spread(nk_ref, 1), axis=1, keepdims=True), LOW)
    top = jnp.maximum(jnp.max(s, axis=1, keepdims=True), jnp.maximum(n0, n1))
    shift = top * FACTOR
    w = jnp.exp2(s * FACTOR - shift)
    w0 = jnp.exp2(n0 * FACTOR - shift)
    w1 = jnp.exp2(n1 * FACTOR - shift)
    total = jnp.sum(w, axis=1, keepdims=True) + w0 + w1
    w = w.astype(BF)
    out = jnp.concatenate(
        [
            jnp.dot(w[k * ROWS:(k + 1) * ROWS], v_ref[i, :, part(g)], preferred_element_type=F32)
            for k, (i, g) in enumerate(pairs)
        ],
        axis=0,
    )
    out += w0.astype(BF).astype(F32) * spread(nv_ref, 0)
    out += w1.astype(BF).astype(F32) * spread(nv_ref, 1)
    o_ref[...] = (out / total).reshape(o_ref.shape)
    lse = top * SCALE + jnp.log(total)
    lane = lax.broadcasted_iota(jnp.int32, (rows, 128), 1)
    lse = jnp.where(lane == row % ROWS, lse, 0.0)
    st_ref[...] = jnp.sum(lse.reshape(len(pairs), ROWS, 128), axis=1).reshape(st_ref.shape)


def own_attention(lengths, q4, keys, values, new_keys, new_values, first, n):
    per = 2
    span = keys.shape[1]
    wide = keys.shape[2]
    skip = first // per
    return pl.pallas_call(
        functools.partial(own_kernel, first=first),
        grid=(n // per,),
        out_shape=(
            jax.ShapeDtypeStruct((n, KVH, ROWS, HD), F32),
            jax.ShapeDtypeStruct((n, KVH, 128), F32),
        ),
        in_specs=[
            pl.BlockSpec(memory_space=pltpu.SMEM),
            pl.BlockSpec((per, KVH, ROWS, HD), lambda i: (i + skip, 0, 0, 0)),
            pl.BlockSpec((per, span, wide), lambda i: (i + skip, 0, 0)),
            pl.BlockSpec((per, span, wide), lambda i: (i + skip, 0, 0)),
            pl.BlockSpec((per, STEPS, wide), lambda i: (i + skip, 0, 0)),
            pl.BlockSpec((per, STEPS, wide), lambda i: (i + skip, 0, 0)),
        ],
        out_specs=(
            pl.BlockSpec((per, KVH, ROWS, HD), lambda i: (i, 0, 0, 0)),
            pl.BlockSpec((per, KVH, 128), lambda i: (i, 0, 0)),
        ),
        compiler_params=pltpu.CompilerParams(vmem_limit_bytes=SMALL_VMEM),
        cost_estimate=pl.CostEstimate(
            flops=4 * n * HEADS * STEPS * span * HD,
            bytes_accessed=2**20 * n // 2,
            transcendentals=0,
        ),
        name="own_attention",
    )(lengths, q4, keys, values, new_keys, new_values)


def flash_kernel(
    x_ref, core_ref, len_ref, q_hbm, a0, a1, a2, a3, b0, b1, b2, b3, out_ref,
    q_ref, kbuf, vbuf, qc, oc, stc, st, acc, tot, mx, bad, pick, posv, poss, sems, psem,
):
    slots = q_ref.shape[0]
    rows = SLOTS * ROWS
    length = len_ref[0]
    x = x_ref[0]
    core = core_ref[0]
    block = a0.shape[1]
    copy_q = pltpu.make_async_copy(q_hbm, q_ref, sems.at[2])
    copy_q.start()
    for half, parts in enumerate(((a0, a1, a2, a3), (b0, b1, b2, b3))):
        side = core if half == 0 else 1 - core
        for d, part in enumerate(parts):
            start = pl.multiple_of((2 * lax.rem(x + d, 4) + side) * block, block)
            pltpu.make_async_copy(part.at[0], kbuf.at[pl.ds(start, block), :], sems.at[0]).start()
            pltpu.make_async_copy(
                part.at[1], vbuf.at[pl.ds(start, block), :], sems.at[1]
            ).start()
    copy_q.wait()
    lane16 = lax.broadcasted_iota(jnp.int32, (16, 128), 1)
    diag = jnp.zeros((16, 128), F32)
    for s in range(slots):
        diag = jnp.where(lane16 == s, q_ref[s, 0:16, :].astype(F32), diag)
    used = jnp.where(diag[0:1, :] < 0.5 * EMPTY, 1.0, 0.0)
    used = jnp.broadcast_to(used, (8, 128))
    r0 = lax.broadcasted_iota(jnp.int32, (128, 128), 0)
    r1 = lax.broadcasted_iota(jnp.int32, (128, 128), 1)
    upper = jnp.where(r0 < r1, 1.0, 0.0).astype(BF)
    before = jnp.dot(used.astype(BF), upper, preferred_element_type=F32)
    sub = lax.broadcasted_iota(jnp.int32, (8, 128), 0)
    posv[...] = jnp.where(sub == 0, before, before + used).astype(jnp.int32)
    copy = pltpu.make_async_copy(posv, poss, psem)
    copy.start()
    p0 = lax.broadcasted_iota(jnp.int32, (3 * rows, 128), 0)
    p1 = lax.broadcasted_iota(jnp.int32, (3 * rows, 128), 1)
    pick[...] = jnp.where(p1 == p0 // rows * ROWS + p0 % ROWS, 1.0, 0.0).astype(BF)
    bad[...] = jnp.zeros(bad.shape, F32)
    copy.wait()
    count = poss[1, 127]

    def gather(s, _):
        qc[pl.ds(pl.multiple_of(poss[0, s] * ROWS, ROWS), ROWS), :] = q_ref[s]
        return 0

    lax.fori_loop(0, slots, gather, 0, unroll=8)
    qc[pl.ds(pl.multiple_of(count * ROWS, ROWS), rows), :] = jnp.zeros((rows, HD), BF)
    pltpu.make_async_copy(kbuf, kbuf, sems.at[0]).wait()
    pltpu.make_async_copy(vbuf, vbuf, sems.at[1]).wait()
    blocks = (count + SLOTS - 1) // SLOTS
    full = length // TILE
    rest = length - full * TILE
    half_tile = rest // (TILE // 2)
    rest = rest - half_tile * (TILE // 2)
    tails = (rest + TAIL - 1) // TAIL

    def values_t(start, size):
        return jnp.concatenate(
            [
                vbuf[pl.ds(pl.multiple_of(start + b * HD, HD), HD), :]
                for b in range(size // HD)
            ],
            axis=1,
        )

    def shift_block(rb, _):
        q = qc[pl.ds(pl.multiple_of(rb * rows, rows), rows), :]
        mx[rb] = jnp.max(dot_t(kbuf[0:SAMPLE, :], q), axis=0, keepdims=True)
        return 0

    lax.fori_loop(0, blocks, shift_block, 0)

    def finish(rb):
        span = pl.ds(pl.multiple_of(rb * rows, rows), rows)
        total = jnp.sum(tot[...], axis=0, keepdims=True)
        bad[...] = jnp.maximum(bad[...], jnp.where(total < LIMIT, 0.0, 1.0))
        oc[span, :] = (acc[...] / total).T.astype(BF)
        lse = mx[rb] * SCALE + jnp.log(total)
        hi = lse.astype(BF)
        low = lse - hi.astype(F32)
        mid = low.astype(BF)
        low = (low - mid.astype(F32)).astype(BF)
        flat = jnp.concatenate([hi, mid, low], axis=1)
        sl = lax.broadcasted_iota(jnp.int32, (SLOTS, 3 * rows), 0)
        ln = lax.broadcasted_iota(jnp.int32, (SLOTS, 3 * rows), 1)
        spread = jnp.where(ln % rows // ROWS == sl, flat.astype(F32), 0.0).astype(BF)
        stc[pl.ds(pl.multiple_of(rb * SLOTS, SLOTS), SLOTS), :] = jnp.dot(
            spread, pick[...], preferred_element_type=F32
        )

    def row_block(rb, _):
        span = pl.ds(pl.multiple_of(rb * rows, rows), rows)

        def fixed(start, size, limit):
            s = dot_t(kbuf[pl.ds(start, size), :], qc[span, :])
            w = jnp.exp2(s * FACTOR - mx[rb] * FACTOR)
            if limit is not None:
                token = lax.broadcasted_iota(jnp.int32, s.shape, 0)
                w = jnp.where(token < limit, w, 0.0)
            tot[...] += jnp.sum(w.reshape(size // 8, 8, rows), axis=0)
            acc[...] += jnp.dot(
                values_t(start, size), w.astype(BF), preferred_element_type=F32
            )

        def fixed_tile(t, _):
            fixed(pl.multiple_of(t * TILE, TILE), TILE, None)
            return 0

        def fixed_half(t, _):
            fixed(pl.multiple_of(full * TILE, TILE), TILE // 2, None)
            return 0

        def fixed_tail(t, _):
            start = full * TILE + half_tile * (TILE // 2) + t * TAIL
            fixed(pl.multiple_of(start, TAIL), TAIL, rest - t * TAIL)
            return 0

        tot[...] = jnp.zeros(tot.shape, F32)
        acc[...] = jnp.zeros(acc.shape, F32)
        lax.fori_loop(0, full, fixed_tile, 0)
        lax.fori_loop(0, half_tile, fixed_half, 0)
        lax.fori_loop(0, tails, fixed_tail, 0)
        finish(rb)
        return 0

    def careful_block(rb, _):
        span = pl.ds(pl.multiple_of(rb * rows, rows), rows)

        def online(t, _):
            start = pl.multiple_of(t * TAIL, TAIL)
            s = dot_t(kbuf[pl.ds(start, TAIL), :], qc[span, :])
            token = lax.broadcasted_iota(jnp.int32, s.shape, 0)
            s = jnp.where(token < length - start, s, LOW)
            old = mx[rb]
            new = jnp.maximum(old, jnp.max(s, axis=0, keepdims=True))
            w = jnp.exp2((s - new) * FACTOR)
            keep = jnp.exp2((old - new) * FACTOR)
            mx[rb] = new
            tot[...] = tot[...] * keep + jnp.sum(w.reshape(TAIL // 8, 8, rows), axis=0)
            acc[...] = acc[...] * keep + jnp.dot(
                values_t(start, TAIL), w.astype(BF), preferred_element_type=F32
            )
            return 0

        mx[rb] = jnp.full((1, rows), LOW, F32)
        tot[...] = jnp.zeros(tot.shape, F32)
        acc[...] = jnp.zeros(acc.shape, F32)
        lax.fori_loop(0, (length + TAIL - 1) // TAIL, online, 0)
        finish(rb)
        return 0

    lax.fori_loop(0, blocks, row_block, 0)

    @pl.when(jnp.max(bad[...]) > 0.0)
    def _():
        lax.fori_loop(0, blocks, careful_block, 0)

    def scatter(s, _):
        p = poss[0, s]
        out_ref[s // CAP, pl.ds(pl.multiple_of((s % CAP) * ROWS, ROWS), ROWS), :] = oc[
            pl.ds(pl.multiple_of(p * ROWS, ROWS), ROWS), :
        ]
        st[s // CAP, pl.ds(s % CAP, 1), :] = stc[pl.ds(p, 1), :]
        return 0

    lax.fori_loop(0, slots, scatter, 0, unroll=8)
    out_ref[:, CAP * ROWS:CAP * ROWS + STATS, :] = st[...].astype(BF)


def prefix_attention(x, core, length, q, parts):
    slots = q.shape[0]
    tokens = 8 * parts[0].shape[1]
    rows = SLOTS * ROWS
    hbm = pl.BlockSpec(memory_space=pl.ANY)
    vmem = pl.BlockSpec(memory_space=pltpu.VMEM)
    return pl.pallas_call(
        flash_kernel,
        out_shape=jax.ShapeDtypeStruct((slots // CAP, CAP * ROWS + STATS, HD), BF),
        in_specs=[pl.BlockSpec(memory_space=pltpu.SMEM)] * 3 + [hbm] * 9,
        out_specs=vmem,
        scratch_shapes=[
            pltpu.VMEM(q.shape, BF),
            pltpu.VMEM((tokens, HD), BF),
            pltpu.VMEM((tokens, HD), BF),
            pltpu.VMEM((slots * ROWS + rows, HD), BF),
            pltpu.VMEM((slots * ROWS, HD), BF),
            pltpu.VMEM((slots, 128), F32),
            pltpu.VMEM((slots // CAP, STATS, 128), F32),
            pltpu.VMEM((HD, rows), F32),
            pltpu.VMEM((8, rows), F32),
            pltpu.VMEM((slots // SLOTS, 1, rows), F32),
            pltpu.VMEM((1, rows), F32),
            pltpu.VMEM((3 * rows, 128), BF),
            pltpu.VMEM((8, 128), jnp.int32),
            pltpu.SMEM((8, 128), jnp.int32),
            pltpu.SemaphoreType.DMA((3,)),
            pltpu.SemaphoreType.DMA,
        ],
        compiler_params=pltpu.CompilerParams(vmem_limit_bytes=VMEM_BYTES),
        cost_estimate=pl.CostEstimate(
            flops=4 * slots * ROWS * tokens * HD, bytes_accessed=8 * 2**20, transcendentals=0
        ),
        name="prefix_attention",
    )(x, core, length, q, *parts)


def combine_kernel(ids_ref, rank_ref, ret_ref, own_a, own_b, st_a, st_b, out_ref):
    lane = lax.broadcasted_iota(jnp.int32, (ROWS, 128), 1)
    row = lax.broadcasted_iota(jnp.int32, (ROWS, 128), 0)
    pick = (lane % ROWS == row) & (lane < 3 * ROWS)
    same = lane == row
    sub = lax.broadcasted_iota(jnp.int32, (STATS, 128), 0)
    for i in range(out_ref.shape[0]):
        p = ids_ref[i]
        j = rank_ref[i]
        start = pl.multiple_of(j * ROWS, ROWS)
        half = own_a.shape[0]
        own, st, k = (own_a, st_a, i) if i < half else (own_b, st_b, i - half)
        for g in range(KVH):
            src = p * KVH + g
            stats = ret_ref[src, CAP * ROWS:CAP * ROWS + STATS, :].astype(F32)
            stats = jnp.sum(jnp.where(sub == j, stats, 0.0), axis=0, keepdims=True)
            lse_p = jnp.sum(jnp.where(pick, stats, 0.0), axis=1, keepdims=True)
            lse_o = jnp.sum(jnp.where(same, st[k, g:g + 1, :], 0.0), axis=1, keepdims=True)
            top = jnp.maximum(lse_p, lse_o)
            wp = jnp.exp(lse_p - top)
            wo = jnp.exp(lse_o - top)
            norm = 1.0 / (wp + wo)
            prefix = ret_ref[src, pl.ds(start, ROWS), :].astype(F32)
            out_ref[i, g] = (wp * norm * prefix + wo * norm * own[k, g]).astype(BF)


def combine(ids, rank, ret, own_a, own_b, st_a, st_b):
    smem = pl.BlockSpec(memory_space=pltpu.SMEM)
    vmem = pl.BlockSpec(memory_space=pltpu.VMEM)
    return pl.pallas_call(
        combine_kernel,
        out_shape=jax.ShapeDtypeStruct((ids.shape[0], KVH, ROWS, HD), BF),
        in_specs=[smem, smem] + [vmem] * 5,
        out_specs=vmem,
        compiler_params=pltpu.CompilerParams(vmem_limit_bytes=SMALL_VMEM),
        name="combine",
    )(ids, rank, ret, own_a, own_b, st_a, st_b)


def on_device(
    queries, new_keys, new_values, suffix_keys, suffix_values, suffix_lengths,
    prefix_of, prefix_keys, prefix_values, prefix_lengths,
):
    n = queries.shape[0]
    x = lax.axis_index("x").astype(jnp.int32).reshape(1)
    core = lax.axis_index("core").astype(jnp.int32).reshape(1)
    moves = {d: [(i, (i + d) % 4) for i in range(4)] for d in (1, 2, 3)}
    q4 = queries.reshape(n, STEPS, HEADS, HD).transpose(0, 2, 1, 3).reshape(n, KVH, ROWS, HD)
    r1, r2, r3, rank, slot = route(x, prefix_of, q4)
    r1, r2, r3, x_late = lax.optimization_barrier((r1, r2, r3, x))
    q3 = lax.ppermute(r1, "x", moves[1])
    q1 = lax.ppermute(r3, "x", moves[3])
    q2 = lax.ppermute(r2, "x", moves[2])
    mine = split_heads(x_late, prefix_keys[0], prefix_values[0])
    parts = [mine[0]] + [lax.ppermute(mine[4 - d], "x", moves[4 - d]) for d in (1, 2, 3)]
    send = pack(x, slot, q4, (q1, q2, q3))
    send, early = lax.optimization_barrier((send, suffix_lengths))
    arrived = lax.all_to_all(send, "prefix", split_axis=0, concat_axis=0, tiled=True)
    own_args = (q4, suffix_keys, suffix_values, new_keys, new_values)
    own_a, st_a = own_attention(early, *own_args, 0, n // 2)
    other = []
    for d in range(4):
        parts[d], st_a = lax.optimization_barrier((parts[d], st_a))
        other.append(lax.ppermute(parts[d], "core", [(0, 1), (1, 0)]))
    back = prefix_attention(
        x, core, prefix_lengths, arrived.reshape(-1, ROWS, HD), parts + other
    )
    back, late = lax.optimization_barrier((back, suffix_lengths))
    ret = lax.all_to_all(back, ("prefix", "x"), split_axis=0, concat_axis=0, tiled=True)
    own_b, st_b = own_attention(late, *own_args, n // 2, n // 2)
    out = combine(prefix_of, rank, ret, own_a, own_b, st_a, st_b)
    out = out.reshape(n, HEADS, STEPS, HD).transpose(0, 2, 1, 3)
    return out.reshape(n, STEPS, HEADS * HD)


def solution(mesh):
    split = Mesh(mesh.devices.reshape(mesh.devices.shape[0], -1, 2), ("prefix", "x", "core"))
    every = ("prefix", "x", "core")
    row = ("x", "core")
    placed = (
        P(every, None, None),
        P(every, None, None),
        P(every, None, None),
        P(every, None, None),
        P(every, None, None),
        P(every),
        P(every),
        P("prefix", row, None),
        P("prefix", row, None),
        P("prefix"),
    )
    return jax.shard_map(
        on_device,
        mesh=split,
        in_specs=placed,
        out_specs=P(every, None, None),
        check_vma=False,
    )
```

```python
import jax
import jax.numpy as jnp
from jax import lax
from jax.experimental import pallas as pl
from jax.experimental.pallas import tpu as pltpu
from jax.sharding import Mesh
from jax.sharding import PartitionSpec as P

F32 = jnp.float32
BF = jnp.bfloat16
HD = 128
CAP = 2
HEADS = 64
KVH = 4
STEPS = 2
GROUP = HEADS // KVH
ROWS = STEPS * GROUP
SCALE = HD ** -0.5
LOG2E = 1.4426950408889634
FACTOR = SCALE * LOG2E
EMPTY = 1024.0
LIMIT = 2.0 ** 100
LOW = -1e30
SLOTS = 16
STATS = 8
TILE = 2048
TAIL = 512
SAMPLE = 256
SMALL_VMEM = 14 * 1024 * 1024
BIG_VMEM = 60 * 1024 * 1024
VMEM_BYTES = 32 * 1024 * 1024


def dot_t(a, b):
    return lax.dot_general(a, b, (((1,), (1,)), ((), ())), preferred_element_type=F32)


def lane_sums(x):
    return sum(x[:, i * 128:(i + 1) * 128] for i in range(x.shape[1] // 128))


def route_kernel(x_ref, ids_ref, q_ref, o0, o1, o2, o3, rank_ref, count, sems):
    x = x_ref[0]
    n = q_ref.shape[0]
    copies = []
    for d, out in enumerate((o0, o1, o2, o3)):
        copy = pltpu.make_async_copy(
            q_ref.at[:, lax.rem(x + d, 4)], out.at[0:n], sems.at[d]
        )
        copy.start()
        copies.append(copy)
    for p in range(16):
        count[p] = 0
    lane = lax.broadcasted_iota(jnp.int32, (ROWS, 128), 1)
    names = jnp.zeros((ROWS, 128), jnp.int32)
    for i in range(n):
        p = ids_ref[i]
        j = count[p]
        count[p] = j + 1
        rank_ref[i] = j
        names = jnp.where(lane == i, p * CAP + j, names)
    names = names.astype(F32).astype(BF)
    for out in (o0, o1, o2, o3):
        out[n] = names
    for copy in copies:
        copy.wait()


def route(x, ids, q4):
    smem = pl.BlockSpec(memory_space=pltpu.SMEM)
    vmem = pl.BlockSpec(memory_space=pltpu.VMEM)
    n = q4.shape[0]
    part = jax.ShapeDtypeStruct((n + 1, ROWS, HD), BF)
    index = jax.ShapeDtypeStruct((n,), jnp.int32)
    return pl.pallas_call(
        route_kernel,
        out_shape=(part,) * 4 + (index,),
        in_specs=[smem, smem, pl.BlockSpec(memory_space=pl.ANY)],
        out_specs=(vmem,) * 4 + (smem,),
        scratch_shapes=[pltpu.SMEM((16,), jnp.int32), pltpu.SemaphoreType.DMA((4,))],
        compiler_params=pltpu.CompilerParams(vmem_limit_bytes=BIG_VMEM),
        name="route",
    )(x, ids, q4)


def pack_kernel(x_ref, p0, p1, p2, p3, out_ref, names, slots, sem):
    x = x_ref[0]
    n = p0.shape[0] - 1
    parts = (p0, p1, p2, p3)
    for d, part in enumerate(parts):
        names[d * 16:d * 16 + 16, :] = part[n, 0:16, :].astype(F32).astype(jnp.int32)
    copy = pltpu.make_async_copy(names, slots, sem)
    copy.start()
    out_ref[...] = jnp.full(out_ref.shape, EMPTY, BF)
    copy.wait()
    for d, part in enumerate(parts):
        source = lax.rem(x + d, 4)
        for i in range(n):
            slot = slots[d * 16, i]
            start = pl.multiple_of(lax.rem(slot, CAP) * ROWS, ROWS)
            out_ref[slot // CAP, source, pl.ds(start, ROWS), :] = part[i]


def pack(x, parts):
    vmem = pl.BlockSpec(memory_space=pltpu.VMEM)
    return pl.pallas_call(
        pack_kernel,
        out_shape=jax.ShapeDtypeStruct((16, 4, CAP * ROWS, HD), BF),
        in_specs=[pl.BlockSpec(memory_space=pltpu.SMEM)] + [vmem] * 4,
        out_specs=vmem,
        scratch_shapes=[
            pltpu.VMEM((64, 128), jnp.int32),
            pltpu.SMEM((64, 128), jnp.int32),
            pltpu.SemaphoreType.DMA,
        ],
        compiler_params=pltpu.CompilerParams(vmem_limit_bytes=SMALL_VMEM),
        name="pack",
    )(x, *parts)


def split_kernel(x_ref, k_ref, v_ref, o0, o1, o2, o3, kbuf, vbuf, tbuf, sems, outs):
    x = x_ref[0]
    order = ((1, o1), (3, o3), (2, o2), (0, o0))
    copies = []
    for d, _ in order:
        column = pl.multiple_of(lax.rem(x + d, 4) * HD, HD)
        copy_v = pltpu.make_async_copy(v_ref.at[:, pl.ds(column, HD)], vbuf.at[d], sems.at[2 * d])
        copy_k = pltpu.make_async_copy(
            k_ref.at[:, pl.ds(column, HD)], kbuf.at[d], sems.at[2 * d + 1]
        )
        copy_v.start()
        copy_k.start()
        copies.append((copy_v, copy_k))
    sends = []
    for (d, out), (copy_v, copy_k) in zip(order, copies):
        copy_v.wait()
        for b in range(vbuf.shape[1] // HD):
            part = slice(b * HD, (b + 1) * HD)
            tbuf[d, part, :] = vbuf[d, part, :].T
        copy_k.wait()
        send_k = pltpu.make_async_copy(kbuf.at[d], out.at[0], outs.at[2 * d])
        send_v = pltpu.make_async_copy(tbuf.at[d], out.at[1], outs.at[2 * d + 1])
        send_k.start()
        send_v.start()
        sends += [send_k, send_v]
    for send in sends:
        send.wait()


def split_heads(x, keys, values):
    hbm = pl.BlockSpec(memory_space=pl.ANY)
    tokens = keys.shape[0]
    shape = jax.ShapeDtypeStruct((2, tokens, HD), BF)
    buf = pltpu.VMEM((4, tokens, HD), BF)
    return pl.pallas_call(
        split_kernel,
        out_shape=(shape,) * 4,
        in_specs=[pl.BlockSpec(memory_space=pltpu.SMEM), hbm, hbm],
        out_specs=(hbm,) * 4,
        scratch_shapes=[
            buf, buf, buf, pltpu.SemaphoreType.DMA((8,)), pltpu.SemaphoreType.DMA((8,))
        ],
        compiler_params=pltpu.CompilerParams(vmem_limit_bytes=BIG_VMEM),
        name="split_heads",
    )(x, keys, values)


def own_kernel(len_ref, q_ref, k_ref, v_ref, nk_ref, nv_ref, o_ref, st_ref):
    per = q_ref.shape[0]
    base = pl.program_id(0) * per
    pairs = [(i, g) for i in range(per) for g in range(KVH)]
    rows = len(pairs) * ROWS

    def part(g):
        return slice(g * HD, (g + 1) * HD)

    def spread(ref, step):
        return jnp.concatenate(
            [
                jnp.broadcast_to(ref[i, step:step + 1, part(g)].astype(F32), (ROWS, HD))
                for i, g in pairs
            ],
            axis=0,
        )

    s = jnp.concatenate([dot_t(q_ref[i, g], k_ref[i, :, part(g)]) for i, g in pairs], axis=0)
    row = lax.broadcasted_iota(jnp.int32, (rows, 1), 0)
    late = row % STEPS >= 1
    limit = jnp.full((rows, 1), len_ref[base], jnp.int32)
    for i in range(1, per):
        limit = jnp.where(row >= i * KVH * ROWS, len_ref[base + i], limit)
    col = lax.broadcasted_iota(jnp.int32, s.shape, 1)
    s = jnp.where(col < limit, s, LOW)
    q = jnp.concatenate([q_ref[i, g] for i, g in pairs], axis=0).astype(F32)
    n0 = jnp.sum(q * spread(nk_ref, 0), axis=1, keepdims=True)
    n1 = jnp.where(late, jnp.sum(q * spread(nk_ref, 1), axis=1, keepdims=True), LOW)
    top = jnp.maximum(jnp.max(s, axis=1, keepdims=True), jnp.maximum(n0, n1))
    shift = top * FACTOR
    w = jnp.exp2(s * FACTOR - shift)
    w0 = jnp.exp2(n0 * FACTOR - shift)
    w1 = jnp.exp2(n1 * FACTOR - shift)
    total = jnp.sum(w, axis=1, keepdims=True) + w0 + w1
    w = w.astype(BF)
    out = jnp.concatenate(
        [
            jnp.dot(w[k * ROWS:(k + 1) * ROWS], v_ref[i, :, part(g)], preferred_element_type=F32)
            for k, (i, g) in enumerate(pairs)
        ],
        axis=0,
    )
    out += w0.astype(BF).astype(F32) * spread(nv_ref, 0)
    out += w1.astype(BF).astype(F32) * spread(nv_ref, 1)
    o_ref[...] = (out / total).reshape(o_ref.shape)
    lse = top * SCALE + jnp.log(total)
    lane = lax.broadcasted_iota(jnp.int32, (rows, 128), 1)
    lse = jnp.where(lane == row % ROWS, lse, 0.0)
    st_ref[...] = jnp.sum(lse.reshape(len(pairs), ROWS, 128), axis=1).reshape(st_ref.shape)


def own_attention(lengths, q4, keys, values, new_keys, new_values):
    n = q4.shape[0]
    per = 2
    span = keys.shape[1]
    wide = keys.shape[2]
    return pl.pallas_call(
        own_kernel,
        grid=(n // per,),
        out_shape=(
            jax.ShapeDtypeStruct((n, KVH, ROWS, HD), F32),
            jax.ShapeDtypeStruct((n, KVH, 128), F32),
        ),
        in_specs=[
            pl.BlockSpec(memory_space=pltpu.SMEM),
            pl.BlockSpec((per, KVH, ROWS, HD), lambda i: (i, 0, 0, 0)),
            pl.BlockSpec((per, span, wide), lambda i: (i, 0, 0)),
            pl.BlockSpec((per, span, wide), lambda i: (i, 0, 0)),
            pl.BlockSpec((per, STEPS, wide), lambda i: (i, 0, 0)),
            pl.BlockSpec((per, STEPS, wide), lambda i: (i, 0, 0)),
        ],
        out_specs=(
            pl.BlockSpec((per, KVH, ROWS, HD), lambda i: (i, 0, 0, 0)),
            pl.BlockSpec((per, KVH, 128), lambda i: (i, 0, 0)),
        ),
        compiler_params=pltpu.CompilerParams(vmem_limit_bytes=BIG_VMEM),
        cost_estimate=pl.CostEstimate(
            flops=4 * n * HEADS * STEPS * span * HD,
            bytes_accessed=2**20 * n // 2,
            transcendentals=0,
        ),
        name="own_attention",
    )(lengths, q4, keys, values, new_keys, new_values)


def flash_kernel(
    x_ref, core_ref, len_ref, q_hbm, a0, a1, a2, a3, b0, b1, b2, b3, out_ref,
    q_ref, kbuf, vbuf, qc, oc, stc, st, acc, tot, mx, bad, pick, posv, poss, sems, psem,
):
    slots = q_ref.shape[0]
    rows = SLOTS * ROWS
    length = len_ref[0]
    x = x_ref[0]
    core = core_ref[0]
    block = a0.shape[1]
    copy_q = pltpu.make_async_copy(q_hbm, q_ref, sems.at[2])
    copy_q.start()
    for half, parts in enumerate(((a0, a1, a2, a3), (b0, b1, b2, b3))):
        side = core if half == 0 else 1 - core
        for d, part in enumerate(parts):
            start = pl.multiple_of((2 * lax.rem(x + d, 4) + side) * block, block)
            pltpu.make_async_copy(part.at[0], kbuf.at[pl.ds(start, block), :], sems.at[0]).start()
            pltpu.make_async_copy(
                part.at[1], vbuf.at[pl.ds(start, block), :], sems.at[1]
            ).start()
    copy_q.wait()
    lane16 = lax.broadcasted_iota(jnp.int32, (16, 128), 1)
    diag = jnp.zeros((16, 128), F32)
    for s in range(slots):
        diag = jnp.where(lane16 == s, q_ref[s, 0:16, :].astype(F32), diag)
    used = jnp.where(diag[0:1, :] < 0.5 * EMPTY, 1.0, 0.0)
    used = jnp.broadcast_to(used, (8, 128))
    r0 = lax.broadcasted_iota(jnp.int32, (128, 128), 0)
    r1 = lax.broadcasted_iota(jnp.int32, (128, 128), 1)
    upper = jnp.where(r0 < r1, 1.0, 0.0).astype(BF)
    before = jnp.dot(used.astype(BF), upper, preferred_element_type=F32)
    sub = lax.broadcasted_iota(jnp.int32, (8, 128), 0)
    posv[...] = jnp.where(sub == 0, before, before + used).astype(jnp.int32)
    copy = pltpu.make_async_copy(posv, poss, psem)
    copy.start()
    p0 = lax.broadcasted_iota(jnp.int32, (3 * rows, 128), 0)
    p1 = lax.broadcasted_iota(jnp.int32, (3 * rows, 128), 1)
    pick[...] = jnp.where(p1 == p0 // rows * ROWS + p0 % ROWS, 1.0, 0.0).astype(BF)
    bad[...] = jnp.zeros(bad.shape, F32)
    copy.wait()
    count = poss[1, 127]

    def gather(s, _):
        qc[pl.ds(pl.multiple_of(poss[0, s] * ROWS, ROWS), ROWS), :] = q_ref[s]
        return 0

    lax.fori_loop(0, slots, gather, 0, unroll=8)
    qc[pl.ds(pl.multiple_of(count * ROWS, ROWS), rows), :] = jnp.zeros((rows, HD), BF)
    pltpu.make_async_copy(kbuf, kbuf, sems.at[0]).wait()
    pltpu.make_async_copy(vbuf, vbuf, sems.at[1]).wait()
    blocks = (count + SLOTS - 1) // SLOTS
    full = length // TILE
    rest = length - full * TILE
    half_tile = rest // (TILE // 2)
    rest = rest - half_tile * (TILE // 2)
    tails = (rest + TAIL - 1) // TAIL

    def values_t(start, size):
        return jnp.concatenate(
            [
                vbuf[pl.ds(pl.multiple_of(start + b * HD, HD), HD), :]
                for b in range(size // HD)
            ],
            axis=1,
        )

    def shift_block(rb, _):
        q = qc[pl.ds(pl.multiple_of(rb * rows, rows), rows), :]
        mx[rb] = jnp.max(dot_t(kbuf[0:SAMPLE, :], q), axis=0, keepdims=True)
        return 0

    lax.fori_loop(0, blocks, shift_block, 0)

    def finish(rb, many):
        wide = many * ROWS
        total = jnp.sum(tot[:, 0:wide], axis=0, keepdims=True)
        bad[:, 0:wide] = jnp.maximum(bad[:, 0:wide], jnp.where(total < LIMIT, 0.0, 1.0))
        oc[pl.ds(pl.multiple_of(rb * rows, rows), wide), :] = (acc[:, 0:wide] / total).T.astype(BF)
        lse = mx[rb, :, 0:wide] * SCALE + jnp.log(total)
        hi = lse.astype(BF)
        low = lse - hi.astype(F32)
        mid = low.astype(BF)
        low = (low - mid.astype(F32)).astype(BF)
        flat = jnp.concatenate([hi, mid, low], axis=1)
        sl = lax.broadcasted_iota(jnp.int32, (many, 3 * wide), 0)
        ln = lax.broadcasted_iota(jnp.int32, (many, 3 * wide), 1)
        spread = jnp.where(ln % wide // ROWS == sl, flat.astype(F32), 0.0).astype(BF)
        chosen = jnp.concatenate([pick[k * rows:k * rows + wide, :] for k in range(3)], axis=0)
        stc[pl.ds(pl.multiple_of(rb * SLOTS, SLOTS), many), :] = jnp.dot(
            spread, chosen, preferred_element_type=F32
        )

    def row_block(rb, many):
        wide = many * ROWS
        span = pl.ds(pl.multiple_of(rb * rows, rows), wide)

        def fixed(start, size, limit):
            s = dot_t(kbuf[pl.ds(start, size), :], qc[span, :])
            w = jnp.exp2(s * FACTOR - mx[rb, :, 0:wide] * FACTOR)
            if limit is not None:
                token = lax.broadcasted_iota(jnp.int32, s.shape, 0)
                w = jnp.where(token < limit, w, 0.0)
            tot[:, 0:wide] += jnp.sum(w.reshape(size // 8, 8, wide), axis=0)
            acc[:, 0:wide] += jnp.dot(
                values_t(start, size), w.astype(BF), preferred_element_type=F32
            )

        def fixed_tile(t, _):
            fixed(pl.multiple_of(t * TILE, TILE), TILE, None)
            return 0

        def fixed_half(t, _):
            fixed(pl.multiple_of(full * TILE, TILE), TILE // 2, None)
            return 0

        def fixed_tail(t, _):
            start = full * TILE + half_tile * (TILE // 2) + t * TAIL
            fixed(pl.multiple_of(start, TAIL), TAIL, rest - t * TAIL)
            return 0

        tot[...] = jnp.zeros(tot.shape, F32)
        acc[...] = jnp.zeros(acc.shape, F32)
        lax.fori_loop(0, full, fixed_tile, 0)
        lax.fori_loop(0, half_tile, fixed_half, 0)
        lax.fori_loop(0, tails, fixed_tail, 0)
        finish(rb, many)
        return 0

    def careful_block(rb, _):
        span = pl.ds(pl.multiple_of(rb * rows, rows), rows)

        def online(t, _):
            start = pl.multiple_of(t * TAIL, TAIL)
            s = dot_t(kbuf[pl.ds(start, TAIL), :], qc[span, :])
            token = lax.broadcasted_iota(jnp.int32, s.shape, 0)
            s = jnp.where(token < length - start, s, LOW)
            old = mx[rb]
            new = jnp.maximum(old, jnp.max(s, axis=0, keepdims=True))
            w = jnp.exp2((s - new) * FACTOR)
            keep = jnp.exp2((old - new) * FACTOR)
            mx[rb] = new
            tot[...] = tot[...] * keep + jnp.sum(w.reshape(TAIL // 8, 8, rows), axis=0)
            acc[...] = acc[...] * keep + jnp.dot(
                values_t(start, TAIL), w.astype(BF), preferred_element_type=F32
            )
            return 0

        mx[rb] = jnp.full((1, rows), LOW, F32)
        tot[...] = jnp.zeros(tot.shape, F32)
        acc[...] = jnp.zeros(acc.shape, F32)
        lax.fori_loop(0, (length + TAIL - 1) // TAIL, online, 0)
        finish(rb, SLOTS)
        return 0

    last = count - count // SLOTS * SLOTS
    whole = count // SLOTS + jnp.where(last > SLOTS // 2, 1, 0)
    lax.fori_loop(0, whole, lambda rb, _: row_block(rb, SLOTS), 0)

    @pl.when((last > 0) & (last <= SLOTS // 2))
    def _():
        row_block(count // SLOTS, SLOTS // 2)

    @pl.when(jnp.max(bad[...]) > 0.0)
    def _():
        lax.fori_loop(0, blocks, careful_block, 0)

    def scatter(s, _):
        p = poss[0, s]
        out_ref[s // CAP, pl.ds(pl.multiple_of((s % CAP) * ROWS, ROWS), ROWS), :] = oc[
            pl.ds(pl.multiple_of(p * ROWS, ROWS), ROWS), :
        ]
        st[s // CAP, pl.ds(s % CAP, 1), :] = stc[pl.ds(p, 1), :]
        return 0

    lax.fori_loop(0, slots, scatter, 0, unroll=8)
    out_ref[:, CAP * ROWS:CAP * ROWS + STATS, :] = st[...].astype(BF)


def prefix_attention(x, core, length, q, parts):
    slots = q.shape[0]
    tokens = 8 * parts[0].shape[1]
    rows = SLOTS * ROWS
    hbm = pl.BlockSpec(memory_space=pl.ANY)
    vmem = pl.BlockSpec(memory_space=pltpu.VMEM)
    return pl.pallas_call(
        flash_kernel,
        out_shape=jax.ShapeDtypeStruct((slots // CAP, CAP * ROWS + STATS, HD), BF),
        in_specs=[pl.BlockSpec(memory_space=pltpu.SMEM)] * 3 + [hbm] * 9,
        out_specs=vmem,
        scratch_shapes=[
            pltpu.VMEM(q.shape, BF),
            pltpu.VMEM((tokens, HD), BF),
            pltpu.VMEM((tokens, HD), BF),
            pltpu.VMEM((slots * ROWS + rows, HD), BF),
            pltpu.VMEM((slots * ROWS, HD), BF),
            pltpu.VMEM((slots, 128), F32),
            pltpu.VMEM((slots // CAP, STATS, 128), F32),
            pltpu.VMEM((HD, rows), F32),
            pltpu.VMEM((8, rows), F32),
            pltpu.VMEM((slots // SLOTS, 1, rows), F32),
            pltpu.VMEM((1, rows), F32),
            pltpu.VMEM((3 * rows, 128), BF),
            pltpu.VMEM((8, 128), jnp.int32),
            pltpu.SMEM((8, 128), jnp.int32),
            pltpu.SemaphoreType.DMA((3,)),
            pltpu.SemaphoreType.DMA,
        ],
        compiler_params=pltpu.CompilerParams(vmem_limit_bytes=VMEM_BYTES),
        cost_estimate=pl.CostEstimate(
            flops=4 * slots * ROWS * tokens * HD, bytes_accessed=8 * 2**20, transcendentals=0
        ),
        name="prefix_attention",
    )(x, core, length, q, *parts)


def combine_kernel(ids_ref, rank_ref, ret_ref, own_ref, st_ref, out_ref, stats):
    n = out_ref.shape[0]
    sub = lax.broadcasted_iota(jnp.int32, (STATS, 128), 0)
    for i in range(n):
        for g in range(KVH):
            rows = ret_ref[ids_ref[i] * KVH + g, CAP * ROWS:CAP * ROWS + STATS, :].astype(F32)
            rows = jnp.where(sub == rank_ref[i], rows, 0.0)
            stats[i * KVH + g:i * KVH + g + 1, :] = jnp.sum(rows, axis=0, keepdims=True)
    lse_p = stats[...]
    lse_p = lse_p + pltpu.roll(lse_p, 128 - ROWS, 1) + pltpu.roll(lse_p, 128 - 2 * ROWS, 1)
    lse_o = st_ref[...]
    top = jnp.maximum(lse_p, lse_o)
    wp = jnp.exp(lse_p - top)
    wo = jnp.exp(lse_o - top)
    stats[...] = wp / (wp + wo)
    lane = lax.broadcasted_iota(jnp.int32, (ROWS, 128), 1)
    row = lax.broadcasted_iota(jnp.int32, (ROWS, 128), 0)
    same = lane == row
    for i in range(n):
        p = ids_ref[i]
        start = pl.multiple_of(rank_ref[i] * ROWS, ROWS)
        for g in range(KVH):
            k = i * KVH + g
            share = jnp.sum(jnp.where(same, stats[k:k + 1, :], 0.0), axis=1, keepdims=True)
            prefix = ret_ref[p * KVH + g, pl.ds(start, ROWS), :].astype(F32)
            own = own_ref[i, g]
            out_ref[i, g] = (own + share * (prefix - own)).astype(BF)


def combine(ids, rank, ret, own, stats):
    smem = pl.BlockSpec(memory_space=pltpu.SMEM)
    vmem = pl.BlockSpec(memory_space=pltpu.VMEM)
    return pl.pallas_call(
        combine_kernel,
        out_shape=jax.ShapeDtypeStruct(own.shape, BF),
        in_specs=[smem, smem, vmem, vmem, vmem],
        out_specs=vmem,
        scratch_shapes=[pltpu.VMEM(stats.shape, F32)],
        compiler_params=pltpu.CompilerParams(vmem_limit_bytes=SMALL_VMEM),
        name="combine",
    )(ids, rank, ret, own, stats)


def on_device(
    queries, new_keys, new_values, suffix_keys, suffix_values, suffix_lengths,
    prefix_of, prefix_keys, prefix_values, prefix_lengths,
):
    n = queries.shape[0]
    x = lax.axis_index("x").astype(jnp.int32).reshape(1)
    core = lax.axis_index("core").astype(jnp.int32).reshape(1)
    moves = {d: [(i, (i + d) % 4) for i in range(4)] for d in (1, 2, 3)}
    q4 = queries.reshape(n, STEPS, HEADS, HD).transpose(0, 2, 1, 3).reshape(n, KVH, ROWS, HD)
    r0, r1, r2, r3, rank = route(x, prefix_of, q4)
    r1, r2, r3, x_late = lax.optimization_barrier((r1, r2, r3, x))
    q3 = lax.ppermute(r1, "x", moves[1])
    q1 = lax.ppermute(r3, "x", moves[3])
    q2 = lax.ppermute(r2, "x", moves[2])
    mine = split_heads(x_late, prefix_keys[0], prefix_values[0])
    parts = [mine[0]] + [lax.ppermute(mine[4 - d], "x", moves[4 - d]) for d in (1, 2, 3)]
    send = pack(x, (r0, q1, q2, q3))
    send, early = lax.optimization_barrier((send, suffix_lengths))
    arrived = lax.all_to_all(send, "prefix", split_axis=0, concat_axis=0, tiled=True)
    own_args = (q4, suffix_keys, suffix_values, new_keys, new_values)
    own, own_stats = own_attention(early, *own_args)
    other = []
    for d in range(4):
        parts[d], own_stats = lax.optimization_barrier((parts[d], own_stats))
        other.append(lax.ppermute(parts[d], "core", [(0, 1), (1, 0)]))
    back = prefix_attention(
        x, core, prefix_lengths, arrived.reshape(-1, ROWS, HD), parts + other
    )
    ret = lax.all_to_all(back, ("prefix", "x"), split_axis=0, concat_axis=0, tiled=True)
    out = combine(prefix_of, rank, ret, own, own_stats.reshape(n * KVH, HD))
    out = out.reshape(n, HEADS, STEPS, HD).transpose(0, 2, 1, 3)
    return out.reshape(n, STEPS, HEADS * HD)


def solution(mesh):
    split = Mesh(mesh.devices.reshape(mesh.devices.shape[0], -1, 2), ("prefix", "x", "core"))
    every = ("prefix", "x", "core")
    row = ("x", "core")
    placed = (
        P(every, None, None),
        P(every, None, None),
        P(every, None, None),
        P(every, None, None),
        P(every, None, None),
        P(every),
        P(every),
        P("prefix", row, None),
        P("prefix", row, None),
        P("prefix"),
    )
    return jax.shard_map(
        on_device,
        mesh=split,
        in_specs=placed,
        out_specs=P(every, None, None),
        check_vma=False,
    )
```

```python
import jax
import jax.numpy as jnp
from jax import lax
from jax.experimental import pallas as pl
from jax.experimental.pallas import tpu as pltpu
from jax.sharding import Mesh
from jax.sharding import PartitionSpec as P

F32 = jnp.float32
BF = jnp.bfloat16
HD = 128
CAP = 2
HEADS = 64
KVH = 4
STEPS = 2
GROUP = HEADS // KVH
ROWS = STEPS * GROUP
SCALE = HD ** -0.5
LOG2E = 1.4426950408889634
FACTOR = SCALE * LOG2E
EMPTY = 1024.0
LIMIT = 2.0 ** 100
LOW = -1e30
SLOTS = 16
STATS = 8
TILES = (4096, 2048, 1024)
TAIL = 512
SAMPLE = 256
SMALL_VMEM = 14 * 1024 * 1024
BIG_VMEM = 60 * 1024 * 1024
VMEM_BYTES = 32 * 1024 * 1024


def dot_t(a, b):
    return lax.dot_general(a, b, (((1,), (1,)), ((), ())), preferred_element_type=F32)


def lane_sums(x):
    return sum(x[:, i * 128:(i + 1) * 128] for i in range(x.shape[1] // 128))


def route_kernel(x_ref, ids_ref, q_ref, o0, o1, o2, o3, rank_ref, count, sems):
    x = x_ref[0]
    n = q_ref.shape[0]
    copies = []
    for d, out in enumerate((o0, o1, o2, o3)):
        copy = pltpu.make_async_copy(
            q_ref.at[:, lax.rem(x + d, 4)], out.at[0:n], sems.at[d]
        )
        copy.start()
        copies.append(copy)
    for p in range(16):
        count[p] = 0
    lane = lax.broadcasted_iota(jnp.int32, (ROWS, 128), 1)
    names = jnp.zeros((ROWS, 128), jnp.int32)
    for i in range(n):
        p = ids_ref[i]
        j = count[p]
        count[p] = j + 1
        rank_ref[i] = j
        names = jnp.where(lane == i, p * CAP + j, names)
    names = names.astype(F32).astype(BF)
    for out in (o0, o1, o2, o3):
        out[n] = names
    for copy in copies:
        copy.wait()


def route(x, ids, q4):
    smem = pl.BlockSpec(memory_space=pltpu.SMEM)
    vmem = pl.BlockSpec(memory_space=pltpu.VMEM)
    n = q4.shape[0]
    part = jax.ShapeDtypeStruct((n + 1, ROWS, HD), BF)
    index = jax.ShapeDtypeStruct((n,), jnp.int32)
    return pl.pallas_call(
        route_kernel,
        out_shape=(part,) * 4 + (index,),
        in_specs=[smem, smem, pl.BlockSpec(memory_space=pl.ANY)],
        out_specs=(vmem,) * 4 + (smem,),
        scratch_shapes=[pltpu.SMEM((16,), jnp.int32), pltpu.SemaphoreType.DMA((4,))],
        compiler_params=pltpu.CompilerParams(vmem_limit_bytes=BIG_VMEM),
        name="route",
    )(x, ids, q4)


def pack_kernel(x_ref, p0, p1, p2, p3, out_ref, names, slots, sem):
    x = x_ref[0]
    n = p0.shape[0] - 1
    parts = (p0, p1, p2, p3)
    for d, part in enumerate(parts):
        names[d * 16:d * 16 + 16, :] = part[n, 0:16, :].astype(F32).astype(jnp.int32)
    copy = pltpu.make_async_copy(names, slots, sem)
    copy.start()
    out_ref[...] = jnp.full(out_ref.shape, EMPTY, BF)
    copy.wait()
    for d, part in enumerate(parts):
        source = lax.rem(x + d, 4)
        for i in range(n):
            slot = slots[d * 16, i]
            start = pl.multiple_of(lax.rem(slot, CAP) * ROWS, ROWS)
            out_ref[slot // CAP, source, pl.ds(start, ROWS), :] = part[i]


def pack(x, parts):
    vmem = pl.BlockSpec(memory_space=pltpu.VMEM)
    return pl.pallas_call(
        pack_kernel,
        out_shape=jax.ShapeDtypeStruct((16, 4, CAP * ROWS, HD), BF),
        in_specs=[pl.BlockSpec(memory_space=pltpu.SMEM)] + [vmem] * 4,
        out_specs=vmem,
        scratch_shapes=[
            pltpu.VMEM((64, 128), jnp.int32),
            pltpu.SMEM((64, 128), jnp.int32),
            pltpu.SemaphoreType.DMA,
        ],
        compiler_params=pltpu.CompilerParams(vmem_limit_bytes=SMALL_VMEM),
        name="pack",
    )(x, *parts)


def split_kernel(x_ref, k_ref, v_ref, o0, o1, o2, o3, kbuf, vbuf, tbuf, sems, outs):
    x = x_ref[0]
    order = ((1, o1), (3, o3), (2, o2), (0, o0))
    copies = []
    for d, _ in order:
        column = pl.multiple_of(lax.rem(x + d, 4) * HD, HD)
        copy_v = pltpu.make_async_copy(v_ref.at[:, pl.ds(column, HD)], vbuf.at[d], sems.at[2 * d])
        copy_k = pltpu.make_async_copy(
            k_ref.at[:, pl.ds(column, HD)], kbuf.at[d], sems.at[2 * d + 1]
        )
        copy_v.start()
        copy_k.start()
        copies.append((copy_v, copy_k))
    sends = []
    for (d, out), (copy_v, copy_k) in zip(order, copies):
        copy_v.wait()
        for b in range(vbuf.shape[1] // HD):
            part = slice(b * HD, (b + 1) * HD)
            tbuf[d, part, :] = vbuf[d, part, :].T
        copy_k.wait()
        send_k = pltpu.make_async_copy(kbuf.at[d], out.at[0], outs.at[2 * d])
        send_v = pltpu.make_async_copy(tbuf.at[d], out.at[1], outs.at[2 * d + 1])
        send_k.start()
        send_v.start()
        sends += [send_k, send_v]
    for send in sends:
        send.wait()


def split_heads(x, keys, values):
    hbm = pl.BlockSpec(memory_space=pl.ANY)
    tokens = keys.shape[0]
    shape = jax.ShapeDtypeStruct((2, tokens, HD), BF)
    buf = pltpu.VMEM((4, tokens, HD), BF)
    return pl.pallas_call(
        split_kernel,
        out_shape=(shape,) * 4,
        in_specs=[pl.BlockSpec(memory_space=pltpu.SMEM), hbm, hbm],
        out_specs=(hbm,) * 4,
        scratch_shapes=[
            buf, buf, buf, pltpu.SemaphoreType.DMA((8,)), pltpu.SemaphoreType.DMA((8,))
        ],
        compiler_params=pltpu.CompilerParams(vmem_limit_bytes=BIG_VMEM),
        name="split_heads",
    )(x, keys, values)


def own_kernel(len_ref, q_ref, k_ref, v_ref, nk_ref, nv_ref, o_ref, st_ref):
    per = q_ref.shape[0]
    base = pl.program_id(0) * per
    pairs = [(i, g) for i in range(per) for g in range(KVH)]
    rows = len(pairs) * ROWS

    def part(g):
        return slice(g * HD, (g + 1) * HD)

    def spread(ref, step):
        return jnp.concatenate(
            [
                jnp.broadcast_to(ref[i, step:step + 1, part(g)].astype(F32), (ROWS, HD))
                for i, g in pairs
            ],
            axis=0,
        )

    s = jnp.concatenate([dot_t(q_ref[i, g], k_ref[i, :, part(g)]) for i, g in pairs], axis=0)
    row = lax.broadcasted_iota(jnp.int32, (rows, 1), 0)
    late = row % STEPS >= 1
    limit = jnp.full((rows, 1), len_ref[base], jnp.int32)
    for i in range(1, per):
        limit = jnp.where(row >= i * KVH * ROWS, len_ref[base + i], limit)
    col = lax.broadcasted_iota(jnp.int32, s.shape, 1)
    s = jnp.where(col < limit, s, LOW)
    q = jnp.concatenate([q_ref[i, g] for i, g in pairs], axis=0).astype(F32)
    n0 = jnp.sum(q * spread(nk_ref, 0), axis=1, keepdims=True)
    n1 = jnp.where(late, jnp.sum(q * spread(nk_ref, 1), axis=1, keepdims=True), LOW)
    top = jnp.maximum(jnp.max(s, axis=1, keepdims=True), jnp.maximum(n0, n1))
    shift = top * FACTOR
    w = jnp.exp2(s * FACTOR - shift)
    w0 = jnp.exp2(n0 * FACTOR - shift)
    w1 = jnp.exp2(n1 * FACTOR - shift)
    total = jnp.sum(w, axis=1, keepdims=True) + w0 + w1
    w = w.astype(BF)
    out = jnp.concatenate(
        [
            jnp.dot(w[k * ROWS:(k + 1) * ROWS], v_ref[i, :, part(g)], preferred_element_type=F32)
            for k, (i, g) in enumerate(pairs)
        ],
        axis=0,
    )
    out += w0.astype(BF).astype(F32) * spread(nv_ref, 0)
    out += w1.astype(BF).astype(F32) * spread(nv_ref, 1)
    o_ref[...] = (out / total).reshape(o_ref.shape)
    lse = top * SCALE + jnp.log(total)
    lane = lax.broadcasted_iota(jnp.int32, (rows, 128), 1)
    lse = jnp.where(lane == row % ROWS, lse, 0.0)
    st_ref[...] = jnp.sum(lse.reshape(len(pairs), ROWS, 128), axis=1).reshape(st_ref.shape)


def own_attention(lengths, q4, keys, values, new_keys, new_values):
    n = q4.shape[0]
    per = 2
    span = keys.shape[1]
    wide = keys.shape[2]
    return pl.pallas_call(
        own_kernel,
        grid=(n // per,),
        out_shape=(
            jax.ShapeDtypeStruct((n, KVH, ROWS, HD), F32),
            jax.ShapeDtypeStruct((n, KVH, 128), F32),
        ),
        in_specs=[
            pl.BlockSpec(memory_space=pltpu.SMEM),
            pl.BlockSpec((per, KVH, ROWS, HD), lambda i: (i, 0, 0, 0)),
            pl.BlockSpec((per, span, wide), lambda i: (i, 0, 0)),
            pl.BlockSpec((per, span, wide), lambda i: (i, 0, 0)),
            pl.BlockSpec((per, STEPS, wide), lambda i: (i, 0, 0)),
            pl.BlockSpec((per, STEPS, wide), lambda i: (i, 0, 0)),
        ],
        out_specs=(
            pl.BlockSpec((per, KVH, ROWS, HD), lambda i: (i, 0, 0, 0)),
            pl.BlockSpec((per, KVH, 128), lambda i: (i, 0, 0)),
        ),
        compiler_params=pltpu.CompilerParams(vmem_limit_bytes=BIG_VMEM),
        cost_estimate=pl.CostEstimate(
            flops=4 * n * HEADS * STEPS * span * HD,
            bytes_accessed=2**20 * n // 2,
            transcendentals=0,
        ),
        name="own_attention",
    )(lengths, q4, keys, values, new_keys, new_values)


def flash_kernel(
    x_ref, core_ref, len_ref, q_hbm, a0, a1, a2, a3, b0, b1, b2, b3, out_ref,
    q_ref, kbuf, vbuf, qc, st, acc, tot, mx, bad, pick, posv, poss, home, sems, psem,
):
    slots = q_ref.shape[0]
    rows = SLOTS * ROWS
    length = len_ref[0]
    x = x_ref[0]
    core = core_ref[0]
    block = a0.shape[1]
    copy_q = pltpu.make_async_copy(q_hbm, q_ref, sems.at[2])
    copy_q.start()
    for half, parts in enumerate(((a0, a1, a2, a3), (b0, b1, b2, b3))):
        side = core if half == 0 else 1 - core
        for d, part in enumerate(parts):
            start = pl.multiple_of((2 * lax.rem(x + d, 4) + side) * block, block)
            pltpu.make_async_copy(part.at[0], kbuf.at[pl.ds(start, block), :], sems.at[0]).start()
            pltpu.make_async_copy(
                part.at[1], vbuf.at[pl.ds(start, block), :], sems.at[1]
            ).start()
    copy_q.wait()
    lane16 = lax.broadcasted_iota(jnp.int32, (16, 128), 1)
    diag = jnp.zeros((16, 128), F32)
    for s in range(slots):
        diag = jnp.where(lane16 == s, q_ref[s, 0:16, :].astype(F32), diag)
    used = jnp.where(diag[0:1, :] < 0.5 * EMPTY, 1.0, 0.0)
    used = jnp.broadcast_to(used, (8, 128))
    r0 = lax.broadcasted_iota(jnp.int32, (128, 128), 0)
    r1 = lax.broadcasted_iota(jnp.int32, (128, 128), 1)
    upper = jnp.where(r0 < r1, 1.0, 0.0).astype(BF)
    before = jnp.dot(used.astype(BF), upper, preferred_element_type=F32)
    sub = lax.broadcasted_iota(jnp.int32, (8, 128), 0)
    posv[...] = jnp.where(sub == 0, before, before + used).astype(jnp.int32)
    copy = pltpu.make_async_copy(posv, poss, psem)
    copy.start()
    p0 = lax.broadcasted_iota(jnp.int32, (3 * rows, 128), 0)
    p1 = lax.broadcasted_iota(jnp.int32, (3 * rows, 128), 1)
    pick[...] = jnp.where(p1 == p0 // rows * ROWS + p0 % ROWS, 1.0, 0.0).astype(BF)
    bad[...] = jnp.zeros(bad.shape, F32)
    copy.wait()
    count = poss[1, 127]

    def gather(s, free):
        p = poss[0, s]
        home[p] = s
        qc[pl.ds(pl.multiple_of(p * ROWS, ROWS), ROWS), :] = q_ref[s]
        return jnp.where(poss[1, s] == p, s, free)

    free = lax.fori_loop(0, slots, gather, 0, unroll=8)
    for k in range(SLOTS):
        home[count + k] = free
    qc[pl.ds(pl.multiple_of(count * ROWS, ROWS), rows), :] = jnp.zeros((rows, HD), BF)
    pltpu.make_async_copy(kbuf, kbuf, sems.at[0]).wait()
    pltpu.make_async_copy(vbuf, vbuf, sems.at[1]).wait()
    blocks = (count + SLOTS - 1) // SLOTS
    plan = []
    done = 0
    for size in TILES:
        many = (length - done) // size
        plan.append((size, done, many))
        done = done + many * size
    rest = length - done
    tails = (rest + TAIL - 1) // TAIL

    def values_t(start, size):
        return jnp.concatenate(
            [
                vbuf[pl.ds(pl.multiple_of(start + b * HD, HD), HD), :]
                for b in range(size // HD)
            ],
            axis=1,
        )

    def shift_block(rb, _):
        q = qc[pl.ds(pl.multiple_of(rb * rows, rows), rows), :]
        mx[rb] = jnp.max(dot_t(kbuf[0:SAMPLE, :], q), axis=0, keepdims=True)
        return 0

    lax.fori_loop(0, blocks, shift_block, 0)

    def finish(rb, many):
        wide = many * ROWS
        total = jnp.sum(tot[:, 0:wide], axis=0, keepdims=True)
        bad[:, 0:wide] = jnp.maximum(bad[:, 0:wide], jnp.where(total < LIMIT, 0.0, 1.0))
        out = (acc[:, 0:wide] / total).T.astype(BF)
        lse = mx[rb, :, 0:wide] * SCALE + jnp.log(total)
        hi = lse.astype(BF)
        low = lse - hi.astype(F32)
        mid = low.astype(BF)
        low = (low - mid.astype(F32)).astype(BF)
        flat = jnp.concatenate([hi, mid, low], axis=1)
        sl = lax.broadcasted_iota(jnp.int32, (many, 3 * wide), 0)
        ln = lax.broadcasted_iota(jnp.int32, (many, 3 * wide), 1)
        spread = jnp.where(ln % wide // ROWS == sl, flat.astype(F32), 0.0).astype(BF)
        chosen = jnp.concatenate([pick[k * rows:k * rows + wide, :] for k in range(3)], axis=0)
        stats = jnp.dot(spread, chosen, preferred_element_type=F32)
        for k in range(many):
            s = home[rb * SLOTS + k]
            start = pl.multiple_of((s % CAP) * ROWS, ROWS)
            out_ref[s // CAP, pl.ds(start, ROWS), :] = out[k * ROWS:(k + 1) * ROWS]
            st[s // CAP, pl.ds(s % CAP, 1), :] = stats[k:k + 1]

    def row_block(rb, many):
        wide = many * ROWS
        span = pl.ds(pl.multiple_of(rb * rows, rows), wide)

        def fixed(start, size, limit):
            s = dot_t(kbuf[pl.ds(start, size), :], qc[span, :])
            w = jnp.exp2(s * FACTOR - mx[rb, :, 0:wide] * FACTOR)
            if limit is not None:
                token = lax.broadcasted_iota(jnp.int32, s.shape, 0)
                w = jnp.where(token < limit, w, 0.0)
            tot[:, 0:wide] += jnp.sum(w.reshape(size // 8, 8, wide), axis=0)
            acc[:, 0:wide] += jnp.dot(
                values_t(start, size), w.astype(BF), preferred_element_type=F32
            )

        def fixed_tail(t, _):
            fixed(pl.multiple_of(done + t * TAIL, TAIL), TAIL, rest - t * TAIL)
            return 0

        def fixed_tiles(size, first):
            def tile(t, _):
                fixed(pl.multiple_of(first + t * size, 1024), size, None)
                return 0

            return tile

        tot[...] = jnp.zeros(tot.shape, F32)
        acc[...] = jnp.zeros(acc.shape, F32)
        for size, first, many_tiles in plan:
            lax.fori_loop(0, many_tiles, fixed_tiles(size, first), 0)
        lax.fori_loop(0, tails, fixed_tail, 0)
        finish(rb, many)
        return 0

    def careful_block(rb, _):
        span = pl.ds(pl.multiple_of(rb * rows, rows), rows)

        def online(t, _):
            start = pl.multiple_of(t * TAIL, TAIL)
            s = dot_t(kbuf[pl.ds(start, TAIL), :], qc[span, :])
            token = lax.broadcasted_iota(jnp.int32, s.shape, 0)
            s = jnp.where(token < length - start, s, LOW)
            old = mx[rb]
            new = jnp.maximum(old, jnp.max(s, axis=0, keepdims=True))
            w = jnp.exp2((s - new) * FACTOR)
            keep = jnp.exp2((old - new) * FACTOR)
            mx[rb] = new
            tot[...] = tot[...] * keep + jnp.sum(w.reshape(TAIL // 8, 8, rows), axis=0)
            acc[...] = acc[...] * keep + jnp.dot(
                values_t(start, TAIL), w.astype(BF), preferred_element_type=F32
            )
            return 0

        mx[rb] = jnp.full((1, rows), LOW, F32)
        tot[...] = jnp.zeros(tot.shape, F32)
        acc[...] = jnp.zeros(acc.shape, F32)
        lax.fori_loop(0, (length + TAIL - 1) // TAIL, online, 0)
        finish(rb, SLOTS)
        return 0

    last = count - count // SLOTS * SLOTS
    whole = count // SLOTS + jnp.where(last > SLOTS // 2, 1, 0)
    lax.fori_loop(0, whole, lambda rb, _: row_block(rb, SLOTS), 0)

    @pl.when((last > 0) & (last <= SLOTS // 2))
    def _():
        row_block(count // SLOTS, SLOTS // 2)

    @pl.when(jnp.max(bad[...]) > 0.0)
    def _():
        lax.fori_loop(0, blocks, careful_block, 0)

    out_ref[:, CAP * ROWS:CAP * ROWS + STATS, :] = st[...].astype(BF)


def prefix_attention(x, core, length, q, parts):
    slots = q.shape[0]
    tokens = 8 * parts[0].shape[1]
    rows = SLOTS * ROWS
    hbm = pl.BlockSpec(memory_space=pl.ANY)
    vmem = pl.BlockSpec(memory_space=pltpu.VMEM)
    return pl.pallas_call(
        flash_kernel,
        out_shape=jax.ShapeDtypeStruct((slots // CAP, CAP * ROWS + STATS, HD), BF),
        in_specs=[pl.BlockSpec(memory_space=pltpu.SMEM)] * 3 + [hbm] * 9,
        out_specs=vmem,
        scratch_shapes=[
            pltpu.VMEM(q.shape, BF),
            pltpu.VMEM((tokens, HD), BF),
            pltpu.VMEM((tokens, HD), BF),
            pltpu.VMEM((slots * ROWS + rows, HD), BF),
            pltpu.VMEM((slots // CAP, STATS, 128), F32),
            pltpu.VMEM((HD, rows), F32),
            pltpu.VMEM((8, rows), F32),
            pltpu.VMEM((slots // SLOTS, 1, rows), F32),
            pltpu.VMEM((1, rows), F32),
            pltpu.VMEM((3 * rows, 128), BF),
            pltpu.VMEM((8, 128), jnp.int32),
            pltpu.SMEM((8, 128), jnp.int32),
            pltpu.SMEM((slots + SLOTS,), jnp.int32),
            pltpu.SemaphoreType.DMA((3,)),
            pltpu.SemaphoreType.DMA,
        ],
        compiler_params=pltpu.CompilerParams(vmem_limit_bytes=VMEM_BYTES),
        cost_estimate=pl.CostEstimate(
            flops=4 * slots * ROWS * tokens * HD, bytes_accessed=8 * 2**20, transcendentals=0
        ),
        name="prefix_attention",
    )(x, core, length, q, *parts)


def combine_kernel(ids_ref, rank_ref, ret_ref, own_ref, st_ref, out_ref, stats):
    n = out_ref.shape[0]
    sub = lax.broadcasted_iota(jnp.int32, (STATS, 128), 0)
    for i in range(n):
        for g in range(KVH):
            rows = ret_ref[ids_ref[i] * KVH + g, CAP * ROWS:CAP * ROWS + STATS, :].astype(F32)
            rows = jnp.where(sub == rank_ref[i], rows, 0.0)
            stats[i * KVH + g:i * KVH + g + 1, :] = jnp.sum(rows, axis=0, keepdims=True)
    lse_p = stats[...]
    lse_p = lse_p + pltpu.roll(lse_p, 128 - ROWS, 1) + pltpu.roll(lse_p, 128 - 2 * ROWS, 1)
    lse_o = st_ref[...]
    top = jnp.maximum(lse_p, lse_o)
    wp = jnp.exp(lse_p - top)
    wo = jnp.exp(lse_o - top)
    stats[...] = wp / (wp + wo)
    lane = lax.broadcasted_iota(jnp.int32, (ROWS, 128), 1)
    row = lax.broadcasted_iota(jnp.int32, (ROWS, 128), 0)
    same = lane == row
    for i in range(n):
        p = ids_ref[i]
        start = pl.multiple_of(rank_ref[i] * ROWS, ROWS)
        for g in range(KVH):
            k = i * KVH + g
            share = jnp.sum(jnp.where(same, stats[k:k + 1, :], 0.0), axis=1, keepdims=True)
            prefix = ret_ref[p * KVH + g, pl.ds(start, ROWS), :].astype(F32)
            own = own_ref[i, g]
            out_ref[i, g] = (own + share * (prefix - own)).astype(BF)


def combine(ids, rank, ret, own, stats):
    smem = pl.BlockSpec(memory_space=pltpu.SMEM)
    vmem = pl.BlockSpec(memory_space=pltpu.VMEM)
    return pl.pallas_call(
        combine_kernel,
        out_shape=jax.ShapeDtypeStruct(own.shape, BF),
        in_specs=[smem, smem, vmem, vmem, vmem],
        out_specs=vmem,
        scratch_shapes=[pltpu.VMEM(stats.shape, F32)],
        compiler_params=pltpu.CompilerParams(vmem_limit_bytes=SMALL_VMEM),
        name="combine",
    )(ids, rank, ret, own, stats)


def on_device(
    queries, new_keys, new_values, suffix_keys, suffix_values, suffix_lengths,
    prefix_of, prefix_keys, prefix_values, prefix_lengths,
):
    n = queries.shape[0]
    x = lax.axis_index("x").astype(jnp.int32).reshape(1)
    core = lax.axis_index("core").astype(jnp.int32).reshape(1)
    moves = {d: [(i, (i + d) % 4) for i in range(4)] for d in (1, 2, 3)}
    q4 = queries.reshape(n, STEPS, HEADS, HD).transpose(0, 2, 1, 3).reshape(n, KVH, ROWS, HD)
    r0, r1, r2, r3, rank = route(x, prefix_of, q4)
    r1, r2, r3, x_late = lax.optimization_barrier((r1, r2, r3, x))
    q3 = lax.ppermute(r1, "x", moves[1])
    q1 = lax.ppermute(r3, "x", moves[3])
    q2 = lax.ppermute(r2, "x", moves[2])
    mine = split_heads(x_late, prefix_keys[0], prefix_values[0])
    parts = [mine[0]] + [lax.ppermute(mine[4 - d], "x", moves[4 - d]) for d in (1, 2, 3)]
    send = pack(x, (r0, q1, q2, q3))
    send, early = lax.optimization_barrier((send, suffix_lengths))
    arrived = lax.all_to_all(send, "prefix", split_axis=0, concat_axis=0, tiled=True)
    own_args = (q4, suffix_keys, suffix_values, new_keys, new_values)
    own, own_stats = own_attention(early, *own_args)
    other = []
    for d in range(4):
        parts[d], own_stats = lax.optimization_barrier((parts[d], own_stats))
        other.append(lax.ppermute(parts[d], "core", [(0, 1), (1, 0)]))
    back = prefix_attention(
        x, core, prefix_lengths, arrived.reshape(-1, ROWS, HD), parts + other
    )
    ret = lax.all_to_all(back, ("prefix", "x"), split_axis=0, concat_axis=0, tiled=True)
    out = combine(prefix_of, rank, ret, own, own_stats.reshape(n * KVH, HD))
    out = out.reshape(n, HEADS, STEPS, HD).transpose(0, 2, 1, 3)
    return out.reshape(n, STEPS, HEADS * HD)


def solution(mesh):
    split = Mesh(mesh.devices.reshape(mesh.devices.shape[0], -1, 2), ("prefix", "x", "core"))
    every = ("prefix", "x", "core")
    row = ("x", "core")
    placed = (
        P(every, None, None),
        P(every, None, None),
        P(every, None, None),
        P(every, None, None),
        P(every, None, None),
        P(every),
        P(every),
        P("prefix", row, None),
        P("prefix", row, None),
        P("prefix"),
    )
    return jax.shard_map(
        on_device,
        mesh=split,
        in_specs=placed,
        out_specs=P(every, None, None),
        check_vma=False,
    )
```

```python
import jax
import jax.numpy as jnp
from jax import lax
from jax.experimental import pallas as pl
from jax.experimental.pallas import tpu as pltpu
from jax.sharding import Mesh
from jax.sharding import PartitionSpec as P

F32 = jnp.float32
BF = jnp.bfloat16
HD = 128
CAP = 2
HEADS = 64
KVH = 4
STEPS = 2
GROUP = HEADS // KVH
ROWS = STEPS * GROUP
SCALE = HD ** -0.5
LOG2E = 1.4426950408889634
FACTOR = SCALE * LOG2E
EMPTY = 1024.0
LIMIT = 2.0 ** 100
LOW = -1e30
SLOTS = 16
STATS = 8
TILES = {32: (4096, 2048, 1024), 16: (4096, 2048, 1024), 8: (4096, 2048, 1024)}
MOST = 32
TAIL = 512
SAMPLE = 256
SMALL_VMEM = 14 * 1024 * 1024
BIG_VMEM = 60 * 1024 * 1024
VMEM_BYTES = 44 * 1024 * 1024


def dot_t(a, b):
    return lax.dot_general(a, b, (((1,), (1,)), ((), ())), preferred_element_type=F32)


def lane_sums(x):
    return sum(x[:, i * 128:(i + 1) * 128] for i in range(x.shape[1] // 128))


def route_kernel(x_ref, ids_ref, q_ref, o0, o1, o2, o3, rank_ref, count, sems):
    x = x_ref[0]
    n = q_ref.shape[0]
    copies = []
    for d, out in enumerate((o0, o1, o2, o3)):
        copy = pltpu.make_async_copy(
            q_ref.at[:, lax.rem(x + d, 4)], out.at[0:n], sems.at[d]
        )
        copy.start()
        copies.append(copy)
    for p in range(16):
        count[p] = 0
    lane = lax.broadcasted_iota(jnp.int32, (ROWS, 128), 1)
    names = jnp.zeros((ROWS, 128), jnp.int32)
    for i in range(n):
        p = ids_ref[i]
        j = count[p]
        count[p] = j + 1
        rank_ref[i] = j
        names = jnp.where(lane == i, p * CAP + j, names)
    names = names.astype(F32).astype(BF)
    for out in (o0, o1, o2, o3):
        out[n] = names
    for copy in copies:
        copy.wait()


def route(x, ids, q4):
    smem = pl.BlockSpec(memory_space=pltpu.SMEM)
    vmem = pl.BlockSpec(memory_space=pltpu.VMEM)
    n = q4.shape[0]
    part = jax.ShapeDtypeStruct((n + 1, ROWS, HD), BF)
    index = jax.ShapeDtypeStruct((n,), jnp.int32)
    return pl.pallas_call(
        route_kernel,
        out_shape=(part,) * 4 + (index,),
        in_specs=[smem, smem, pl.BlockSpec(memory_space=pl.ANY)],
        out_specs=(vmem,) * 4 + (smem,),
        scratch_shapes=[pltpu.SMEM((16,), jnp.int32), pltpu.SemaphoreType.DMA((4,))],
        compiler_params=pltpu.CompilerParams(vmem_limit_bytes=BIG_VMEM),
        name="route",
    )(x, ids, q4)


def pack_kernel(x_ref, p0, p1, p2, p3, out_ref, names, slots, sem):
    x = x_ref[0]
    n = p0.shape[0] - 1
    parts = (p0, p1, p2, p3)
    for d, part in enumerate(parts):
        names[d * 16:d * 16 + 16, :] = part[n, 0:16, :].astype(F32).astype(jnp.int32)
    copy = pltpu.make_async_copy(names, slots, sem)
    copy.start()
    out_ref[...] = jnp.full(out_ref.shape, EMPTY, BF)
    copy.wait()
    for d, part in enumerate(parts):
        source = lax.rem(x + d, 4)
        for i in range(n):
            slot = slots[d * 16, i]
            start = pl.multiple_of(lax.rem(slot, CAP) * ROWS, ROWS)
            out_ref[slot // CAP, source, pl.ds(start, ROWS), :] = part[i]


def pack(x, parts):
    vmem = pl.BlockSpec(memory_space=pltpu.VMEM)
    return pl.pallas_call(
        pack_kernel,
        out_shape=jax.ShapeDtypeStruct((16, 4, CAP * ROWS, HD), BF),
        in_specs=[pl.BlockSpec(memory_space=pltpu.SMEM)] + [vmem] * 4,
        out_specs=vmem,
        scratch_shapes=[
            pltpu.VMEM((64, 128), jnp.int32),
            pltpu.SMEM((64, 128), jnp.int32),
            pltpu.SemaphoreType.DMA,
        ],
        compiler_params=pltpu.CompilerParams(vmem_limit_bytes=SMALL_VMEM),
        name="pack",
    )(x, *parts)


def split_kernel(x_ref, k_ref, v_ref, o0, o1, o2, o3, kbuf, vbuf, tbuf, sems, outs):
    x = x_ref[0]
    order = ((1, o1), (3, o3), (2, o2), (0, o0))
    copies = []
    for d, _ in order:
        column = pl.multiple_of(lax.rem(x + d, 4) * HD, HD)
        copy_v = pltpu.make_async_copy(v_ref.at[:, pl.ds(column, HD)], vbuf.at[d], sems.at[2 * d])
        copy_k = pltpu.make_async_copy(
            k_ref.at[:, pl.ds(column, HD)], kbuf.at[d], sems.at[2 * d + 1]
        )
        copy_v.start()
        copy_k.start()
        copies.append((copy_v, copy_k))
    sends = []
    for (d, out), (copy_v, copy_k) in zip(order, copies):
        copy_v.wait()
        for b in range(vbuf.shape[1] // HD):
            part = slice(b * HD, (b + 1) * HD)
            tbuf[d, part, :] = vbuf[d, part, :].T
        copy_k.wait()
        send_k = pltpu.make_async_copy(kbuf.at[d], out.at[0], outs.at[2 * d])
        send_v = pltpu.make_async_copy(tbuf.at[d], out.at[1], outs.at[2 * d + 1])
        send_k.start()
        send_v.start()
        sends += [send_k, send_v]
    for send in sends:
        send.wait()


def split_heads(x, keys, values):
    hbm = pl.BlockSpec(memory_space=pl.ANY)
    tokens = keys.shape[0]
    shape = jax.ShapeDtypeStruct((2, tokens, HD), BF)
    buf = pltpu.VMEM((4, tokens, HD), BF)
    return pl.pallas_call(
        split_kernel,
        out_shape=(shape,) * 4,
        in_specs=[pl.BlockSpec(memory_space=pltpu.SMEM), hbm, hbm],
        out_specs=(hbm,) * 4,
        scratch_shapes=[
            buf, buf, buf, pltpu.SemaphoreType.DMA((8,)), pltpu.SemaphoreType.DMA((8,))
        ],
        compiler_params=pltpu.CompilerParams(vmem_limit_bytes=BIG_VMEM),
        name="split_heads",
    )(x, keys, values)


def own_kernel(len_ref, q_ref, k_ref, v_ref, nk_ref, nv_ref, o_ref, st_ref):
    per = q_ref.shape[0]
    base = pl.program_id(0) * per
    pairs = [(i, g) for i in range(per) for g in range(KVH)]
    rows = len(pairs) * ROWS

    def part(g):
        return slice(g * HD, (g + 1) * HD)

    def spread(ref, step):
        return jnp.concatenate(
            [
                jnp.broadcast_to(ref[i, step:step + 1, part(g)].astype(F32), (ROWS, HD))
                for i, g in pairs
            ],
            axis=0,
        )

    s = jnp.concatenate([dot_t(q_ref[i, g], k_ref[i, :, part(g)]) for i, g in pairs], axis=0)
    row = lax.broadcasted_iota(jnp.int32, (rows, 1), 0)
    late = row % STEPS >= 1
    limit = jnp.full((rows, 1), len_ref[base], jnp.int32)
    for i in range(1, per):
        limit = jnp.where(row >= i * KVH * ROWS, len_ref[base + i], limit)
    col = lax.broadcasted_iota(jnp.int32, s.shape, 1)
    s = jnp.where(col < limit, s, LOW)
    q = jnp.concatenate([q_ref[i, g] for i, g in pairs], axis=0).astype(F32)
    n0 = jnp.sum(q * spread(nk_ref, 0), axis=1, keepdims=True)
    n1 = jnp.where(late, jnp.sum(q * spread(nk_ref, 1), axis=1, keepdims=True), LOW)
    top = jnp.maximum(jnp.max(s, axis=1, keepdims=True), jnp.maximum(n0, n1))
    shift = top * FACTOR
    w = jnp.exp2(s * FACTOR - shift)
    w0 = jnp.exp2(n0 * FACTOR - shift)
    w1 = jnp.exp2(n1 * FACTOR - shift)
    total = jnp.sum(w, axis=1, keepdims=True) + w0 + w1
    w = w.astype(BF)
    out = jnp.concatenate(
        [
            jnp.dot(w[k * ROWS:(k + 1) * ROWS], v_ref[i, :, part(g)], preferred_element_type=F32)
            for k, (i, g) in enumerate(pairs)
        ],
        axis=0,
    )
    out += w0.astype(BF).astype(F32) * spread(nv_ref, 0)
    out += w1.astype(BF).astype(F32) * spread(nv_ref, 1)
    o_ref[...] = (out / total).reshape(o_ref.shape)
    lse = top * SCALE + jnp.log(total)
    lane = lax.broadcasted_iota(jnp.int32, (rows, 128), 1)
    lse = jnp.where(lane == row % ROWS, lse, 0.0)
    st_ref[...] = jnp.sum(lse.reshape(len(pairs), ROWS, 128), axis=1).reshape(st_ref.shape)


def own_attention(lengths, q4, keys, values, new_keys, new_values):
    n = q4.shape[0]
    per = 2
    span = keys.shape[1]
    wide = keys.shape[2]
    return pl.pallas_call(
        own_kernel,
        grid=(n // per,),
        out_shape=(
            jax.ShapeDtypeStruct((n, KVH, ROWS, HD), F32),
            jax.ShapeDtypeStruct((n, KVH, 128), F32),
        ),
        in_specs=[
            pl.BlockSpec(memory_space=pltpu.SMEM),
            pl.BlockSpec((per, KVH, ROWS, HD), lambda i: (i, 0, 0, 0)),
            pl.BlockSpec((per, span, wide), lambda i: (i, 0, 0)),
            pl.BlockSpec((per, span, wide), lambda i: (i, 0, 0)),
            pl.BlockSpec((per, STEPS, wide), lambda i: (i, 0, 0)),
            pl.BlockSpec((per, STEPS, wide), lambda i: (i, 0, 0)),
        ],
        out_specs=(
            pl.BlockSpec((per, KVH, ROWS, HD), lambda i: (i, 0, 0, 0)),
            pl.BlockSpec((per, KVH, 128), lambda i: (i, 0, 0)),
        ),
        compiler_params=pltpu.CompilerParams(vmem_limit_bytes=BIG_VMEM),
        cost_estimate=pl.CostEstimate(
            flops=4 * n * HEADS * STEPS * span * HD,
            bytes_accessed=2**20 * n // 2,
            transcendentals=0,
        ),
        name="own_attention",
    )(lengths, q4, keys, values, new_keys, new_values)


def flash_kernel(
    x_ref, core_ref, len_ref, q_hbm, a0, a1, a2, a3, b0, b1, b2, b3, out_ref,
    q_ref, kbuf, vbuf, qc, st, acc, tot, mx, bad, pick, posv, poss, home, sems, psem,
):
    slots = q_ref.shape[0]
    rows = SLOTS * ROWS
    most = MOST * ROWS
    length = len_ref[0]
    x = x_ref[0]
    core = core_ref[0]
    block = a0.shape[1]
    copy_q = pltpu.make_async_copy(q_hbm, q_ref, sems.at[2])
    copy_q.start()
    for half, parts in enumerate(((a0, a1, a2, a3), (b0, b1, b2, b3))):
        side = core if half == 0 else 1 - core
        for d, part in enumerate(parts):
            start = pl.multiple_of((2 * lax.rem(x + d, 4) + side) * block, block)
            pltpu.make_async_copy(part.at[0], kbuf.at[pl.ds(start, block), :], sems.at[0]).start()
            pltpu.make_async_copy(
                part.at[1], vbuf.at[pl.ds(start, block), :], sems.at[1]
            ).start()
    copy_q.wait()
    lane16 = lax.broadcasted_iota(jnp.int32, (16, 128), 1)
    diag = jnp.zeros((16, 128), F32)
    for s in range(slots):
        diag = jnp.where(lane16 == s, q_ref[s, 0:16, :].astype(F32), diag)
    used = jnp.where(diag[0:1, :] < 0.5 * EMPTY, 1.0, 0.0)
    used = jnp.broadcast_to(used, (8, 128))
    r0 = lax.broadcasted_iota(jnp.int32, (128, 128), 0)
    r1 = lax.broadcasted_iota(jnp.int32, (128, 128), 1)
    upper = jnp.where(r0 < r1, 1.0, 0.0).astype(BF)
    before = jnp.dot(used.astype(BF), upper, preferred_element_type=F32)
    sub = lax.broadcasted_iota(jnp.int32, (8, 128), 0)
    posv[...] = jnp.where(sub == 0, before, before + used).astype(jnp.int32)
    copy = pltpu.make_async_copy(posv, poss, psem)
    copy.start()
    p0 = lax.broadcasted_iota(jnp.int32, (3 * most, 128), 0)
    p1 = lax.broadcasted_iota(jnp.int32, (3 * most, 128), 1)
    pick[...] = jnp.where(p1 == p0 // most * ROWS + p0 % ROWS, 1.0, 0.0).astype(BF)
    bad[...] = jnp.zeros(bad.shape, F32)
    copy.wait()
    count = poss[1, 127]

    def gather(s, free):
        p = poss[0, s]
        home[p] = s
        qc[pl.ds(pl.multiple_of(p * ROWS, ROWS), ROWS), :] = q_ref[s]
        return jnp.where(poss[1, s] == p, s, free)

    free = lax.fori_loop(0, slots, gather, 0, unroll=8)
    for k in range(SLOTS):
        home[count + k] = free
    qc[pl.ds(pl.multiple_of(count * ROWS, ROWS), rows), :] = jnp.zeros((rows, HD), BF)
    pltpu.make_async_copy(kbuf, kbuf, sems.at[0]).wait()
    pltpu.make_async_copy(vbuf, vbuf, sems.at[1]).wait()
    blocks = (count + SLOTS - 1) // SLOTS
    plans = {}
    for many, sizes in TILES.items():
        plan = []
        done = 0
        for size in sizes:
            tiles = (length - done) // size
            plan.append((size, done, tiles))
            done = done + tiles * size
        plans[many] = (plan, done, length - done)

    def values_t(start, size):
        return jnp.concatenate(
            [
                vbuf[pl.ds(pl.multiple_of(start + b * HD, HD), HD), :]
                for b in range(size // HD)
            ],
            axis=1,
        )

    def lanes(first, many):
        return pl.ds(pl.multiple_of(first * ROWS, 8 * ROWS), many * ROWS)

    def shift_block(rb, _):
        q = qc[pl.ds(pl.multiple_of(rb * rows, rows), rows), :]
        mx[:, lanes(rb * SLOTS, SLOTS)] = jnp.max(
            dot_t(kbuf[0:SAMPLE, :], q), axis=0, keepdims=True
        )
        return 0

    lax.fori_loop(0, blocks, shift_block, 0)

    def finish(first, many):
        wide = many * ROWS
        total = jnp.sum(tot[:, 0:wide], axis=0, keepdims=True)
        bad[:, 0:wide] = jnp.maximum(bad[:, 0:wide], jnp.where(total < LIMIT, 0.0, 1.0))
        out = (acc[:, 0:wide] / total).T.astype(BF)
        lse = mx[:, lanes(first, many)] * SCALE + jnp.log(total)
        hi = lse.astype(BF)
        low = lse - hi.astype(F32)
        mid = low.astype(BF)
        low = (low - mid.astype(F32)).astype(BF)
        flat = jnp.concatenate([hi, mid, low], axis=1)
        sl = lax.broadcasted_iota(jnp.int32, (many, 3 * wide), 0)
        ln = lax.broadcasted_iota(jnp.int32, (many, 3 * wide), 1)
        spread = jnp.where(ln % wide // ROWS == sl, flat.astype(F32), 0.0).astype(BF)
        chosen = jnp.concatenate([pick[k * most:k * most + wide, :] for k in range(3)], axis=0)
        stats = jnp.dot(spread, chosen, preferred_element_type=F32)
        for k in range(many):
            s = home[first + k]
            start = pl.multiple_of((s % CAP) * ROWS, ROWS)
            out_ref[s // CAP, pl.ds(start, ROWS), :] = out[k * ROWS:(k + 1) * ROWS]
            st[s // CAP, pl.ds(s % CAP, 1), :] = stats[k:k + 1]

    def row_block(first, many):
        wide = many * ROWS
        span = lanes(first, many)
        plan, done, rest = plans[many]
        tails = (rest + TAIL - 1) // TAIL

        def fixed(start, size, limit):
            s = dot_t(kbuf[pl.ds(start, size), :], qc[span, :])
            w = jnp.exp2(s * FACTOR - mx[:, span] * FACTOR)
            if limit is not None:
                token = lax.broadcasted_iota(jnp.int32, s.shape, 0)
                w = jnp.where(token < limit, w, 0.0)
            tot[:, 0:wide] += jnp.sum(w.reshape(size // 8, 8, wide), axis=0)
            acc[:, 0:wide] += jnp.dot(
                values_t(start, size), w.astype(BF), preferred_element_type=F32
            )

        def fixed_tail(t, _):
            fixed(pl.multiple_of(done + t * TAIL, TAIL), TAIL, rest - t * TAIL)
            return 0

        def fixed_tiles(size, begin):
            def tile(t, _):
                fixed(pl.multiple_of(begin + t * size, 1024), size, None)
                return 0

            return tile

        tot[:, 0:wide] = jnp.zeros((8, wide), F32)
        acc[:, 0:wide] = jnp.zeros((HD, wide), F32)
        for size, begin, tiles in plan:
            lax.fori_loop(0, tiles, fixed_tiles(size, begin), 0)
        lax.fori_loop(0, tails, fixed_tail, 0)
        finish(first, many)
        return 0

    def careful_block(rb, _):
        span = lanes(rb * SLOTS, SLOTS)

        def online(t, _):
            start = pl.multiple_of(t * TAIL, TAIL)
            s = dot_t(kbuf[pl.ds(start, TAIL), :], qc[span, :])
            token = lax.broadcasted_iota(jnp.int32, s.shape, 0)
            s = jnp.where(token < length - start, s, LOW)
            old = mx[:, span]
            new = jnp.maximum(old, jnp.max(s, axis=0, keepdims=True))
            w = jnp.exp2((s - new) * FACTOR)
            keep = jnp.exp2((old - new) * FACTOR)
            mx[:, span] = new
            tot[:, 0:rows] = tot[:, 0:rows] * keep + jnp.sum(w.reshape(TAIL // 8, 8, rows), axis=0)
            acc[:, 0:rows] = acc[:, 0:rows] * keep + jnp.dot(
                values_t(start, TAIL), w.astype(BF), preferred_element_type=F32
            )
            return 0

        mx[:, span] = jnp.full((1, rows), LOW, F32)
        tot[:, 0:rows] = jnp.zeros((8, rows), F32)
        acc[:, 0:rows] = jnp.zeros((HD, rows), F32)
        lax.fori_loop(0, (length + TAIL - 1) // TAIL, online, 0)
        finish(rb * SLOTS, SLOTS)
        return 0

    last = lax.rem(count, MOST)
    base = count - last
    most_blocks = base // MOST + jnp.where(last > 24, 1, 0)
    lax.fori_loop(0, most_blocks, lambda rb, _: row_block(rb * MOST, MOST), 0)

    @pl.when((last > 8) & (last <= 24))
    def _():
        row_block(base, 16)

    @pl.when((last > 0) & (last <= 8))
    def _():
        row_block(base, 8)

    @pl.when((last > 16) & (last <= 24))
    def _():
        row_block(base + 16, 8)

    @pl.when(jnp.max(bad[...]) > 0.0)
    def _():
        lax.fori_loop(0, blocks, careful_block, 0)

    out_ref[:, CAP * ROWS:CAP * ROWS + STATS, :] = st[...].astype(BF)


def prefix_attention(x, core, length, q, parts):
    slots = q.shape[0]
    tokens = 8 * parts[0].shape[1]
    rows = SLOTS * ROWS
    hbm = pl.BlockSpec(memory_space=pl.ANY)
    vmem = pl.BlockSpec(memory_space=pltpu.VMEM)
    return pl.pallas_call(
        flash_kernel,
        out_shape=jax.ShapeDtypeStruct((slots // CAP, CAP * ROWS + STATS, HD), BF),
        in_specs=[pl.BlockSpec(memory_space=pltpu.SMEM)] * 3 + [hbm] * 9,
        out_specs=vmem,
        scratch_shapes=[
            pltpu.VMEM(q.shape, BF),
            pltpu.VMEM((tokens, HD), BF),
            pltpu.VMEM((tokens, HD), BF),
            pltpu.VMEM((slots * ROWS + rows, HD), BF),
            pltpu.VMEM((slots // CAP, STATS, 128), F32),
            pltpu.VMEM((HD, MOST * ROWS), F32),
            pltpu.VMEM((8, MOST * ROWS), F32),
            pltpu.VMEM((1, slots * ROWS), F32),
            pltpu.VMEM((1, MOST * ROWS), F32),
            pltpu.VMEM((3 * MOST * ROWS, 128), BF),
            pltpu.VMEM((8, 128), jnp.int32),
            pltpu.SMEM((8, 128), jnp.int32),
            pltpu.SMEM((slots + SLOTS,), jnp.int32),
            pltpu.SemaphoreType.DMA((3,)),
            pltpu.SemaphoreType.DMA,
        ],
        compiler_params=pltpu.CompilerParams(vmem_limit_bytes=VMEM_BYTES),
        cost_estimate=pl.CostEstimate(
            flops=4 * slots * ROWS * tokens * HD, bytes_accessed=8 * 2**20, transcendentals=0
        ),
        name="prefix_attention",
    )(x, core, length, q, *parts)


def combine_kernel(ids_ref, rank_ref, ret_ref, own_ref, st_ref, out_ref, stats):
    n = out_ref.shape[0]
    sub = lax.broadcasted_iota(jnp.int32, (STATS, 128), 0)
    for i in range(n):
        for g in range(KVH):
            rows = ret_ref[ids_ref[i] * KVH + g, CAP * ROWS:CAP * ROWS + STATS, :].astype(F32)
            rows = jnp.where(sub == rank_ref[i], rows, 0.0)
            stats[i * KVH + g:i * KVH + g + 1, :] = jnp.sum(rows, axis=0, keepdims=True)
    lse_p = stats[...]
    lse_p = lse_p + pltpu.roll(lse_p, 128 - ROWS, 1) + pltpu.roll(lse_p, 128 - 2 * ROWS, 1)
    lse_o = st_ref[...]
    top = jnp.maximum(lse_p, lse_o)
    wp = jnp.exp(lse_p - top)
    wo = jnp.exp(lse_o - top)
    stats[...] = wp / (wp + wo)
    lane = lax.broadcasted_iota(jnp.int32, (ROWS, 128), 1)
    row = lax.broadcasted_iota(jnp.int32, (ROWS, 128), 0)
    same = lane == row
    for i in range(n):
        p = ids_ref[i]
        start = pl.multiple_of(rank_ref[i] * ROWS, ROWS)
        for g in range(KVH):
            k = i * KVH + g
            share = jnp.sum(jnp.where(same, stats[k:k + 1, :], 0.0), axis=1, keepdims=True)
            prefix = ret_ref[p * KVH + g, pl.ds(start, ROWS), :].astype(F32)
            own = own_ref[i, g]
            out_ref[i, g] = (own + share * (prefix - own)).astype(BF)


def combine(ids, rank, ret, own, stats):
    smem = pl.BlockSpec(memory_space=pltpu.SMEM)
    vmem = pl.BlockSpec(memory_space=pltpu.VMEM)
    return pl.pallas_call(
        combine_kernel,
        out_shape=jax.ShapeDtypeStruct(own.shape, BF),
        in_specs=[smem, smem, vmem, vmem, vmem],
        out_specs=vmem,
        scratch_shapes=[pltpu.VMEM(stats.shape, F32)],
        compiler_params=pltpu.CompilerParams(vmem_limit_bytes=SMALL_VMEM),
        name="combine",
    )(ids, rank, ret, own, stats)


def on_device(
    queries, new_keys, new_values, suffix_keys, suffix_values, suffix_lengths,
    prefix_of, prefix_keys, prefix_values, prefix_lengths,
):
    n = queries.shape[0]
    x = lax.axis_index("x").astype(jnp.int32).reshape(1)
    core = lax.axis_index("core").astype(jnp.int32).reshape(1)
    moves = {d: [(i, (i + d) % 4) for i in range(4)] for d in (1, 2, 3)}
    q4 = queries.reshape(n, STEPS, HEADS, HD).transpose(0, 2, 1, 3).reshape(n, KVH, ROWS, HD)
    r0, r1, r2, r3, rank = route(x, prefix_of, q4)
    r1, r2, r3, x_late = lax.optimization_barrier((r1, r2, r3, x))
    q3 = lax.ppermute(r1, "x", moves[1])
    q1 = lax.ppermute(r3, "x", moves[3])
    q2 = lax.ppermute(r2, "x", moves[2])
    mine = split_heads(x_late, prefix_keys[0], prefix_values[0])
    parts = [mine[0]] + [lax.ppermute(mine[4 - d], "x", moves[4 - d]) for d in (1, 2, 3)]
    send = pack(x, (r0, q1, q2, q3))
    send, early = lax.optimization_barrier((send, suffix_lengths))
    arrived = lax.all_to_all(send, "prefix", split_axis=0, concat_axis=0, tiled=True)
    own_args = (q4, suffix_keys, suffix_values, new_keys, new_values)
    own, own_stats = own_attention(early, *own_args)
    other = []
    for d in range(4):
        parts[d], own_stats = lax.optimization_barrier((parts[d], own_stats))
        other.append(lax.ppermute(parts[d], "core", [(0, 1), (1, 0)]))
    back = prefix_attention(
        x, core, prefix_lengths, arrived.reshape(-1, ROWS, HD), parts + other
    )
    ret = lax.all_to_all(back, ("prefix", "x"), split_axis=0, concat_axis=0, tiled=True)
    out = combine(prefix_of, rank, ret, own, own_stats.reshape(n * KVH, HD))
    out = out.reshape(n, HEADS, STEPS, HD).transpose(0, 2, 1, 3)
    return out.reshape(n, STEPS, HEADS * HD)


def solution(mesh):
    split = Mesh(mesh.devices.reshape(mesh.devices.shape[0], -1, 2), ("prefix", "x", "core"))
    every = ("prefix", "x", "core")
    row = ("x", "core")
    placed = (
        P(every, None, None),
        P(every, None, None),
        P(every, None, None),
        P(every, None, None),
        P(every, None, None),
        P(every),
        P(every),
        P("prefix", row, None),
        P("prefix", row, None),
        P("prefix"),
    )
    return jax.shard_map(
        on_device,
        mesh=split,
        in_specs=placed,
        out_specs=P(every, None, None),
        check_vma=False,
    )
```
